32 devices in a mesh: ctx: 4 (over z), seq: 2 (over y), ch: 4 (over x, core).
Axes of the slice: x: 2, y: 2, z: 4, core: 2. Of those that a mesh axis runs over, the one named last changes fastest.
Arguments:
- grad_out: float32 [2, 512, 2048], P('seq', 'ch', 'ctx'), may hold values from -6 to 6
- query: float32 [2, 512, 2048], P('seq', 'ch', 'ctx'), may hold values from -6 to 6
- keys: float32 [2, 512, 2048], P('seq', 'ch', 'ctx'), may hold values from -6 to 6
- values: float32 [2, 512, 2048], P('seq', 'ch', 'ctx'), may hold values from -6 to 6
- long_filter: float32 [512, 2048], P(('ch', 'ctx')), may hold values from -6 to 6
- short_filter: float32 [512, 3], P('ch'), may hold values from -3.5 to 3.5
Outputs:
- grad_query: float32 [2, 512, 2048], P('seq', 'ch', 'ctx')
- grad_keys: float32 [2, 512, 2048], P('seq', 'ch', 'ctx')
- grad_values: float32 [2, 512, 2048], P('seq', 'ch', 'ctx')
- grad_long: float32 [512, 2048], P(('ch', 'ctx'))
The draws below stay inside these ranges and needn't reach their ends.
All inputs are finite; a program needn't handle non-finite values.
Results may differ from the reference program's by a relative error of at most 0.0001.
Values sent between devices are 32-bit elements; how exact they have to be, the bound alone decides.
A program may use at most 64 MiB of HBM per device.

```python
import jax
import jax.numpy as jnp
from jax import lax

TAPS = 3
CHANNELS = 512
SEQ_LEN = 2048
SEQS = 2


def levels(key, extent, cuts, low, largest):
    factor_of, own = 1.0, jax.random.fold_in(key, 6)
    for position, blocks in cuts:
        heights = jnp.exp(jax.random.uniform(jax.random.fold_in(own, position), (blocks,), jnp.float32, low / len(cuts), largest / len(cuts)))
        factor_of = factor_of * jnp.repeat(heights, extent[position] // blocks).reshape([-1 if axis == position else 1 for axis in range(len(extent))])
    return factor_of


def centred(key, shape, deviation, limit, cuts=(), held_as=jnp.bfloat16):
    loudness = levels(key, shape, cuts, -0.22, 0.18) if cuts else 1.0
    result = jax.random.normal(key, shape, jnp.float32) * deviation * loudness
    return jnp.minimum(jnp.maximum(result, -limit), limit).astype(held_as)


def setup_inputs(seed: int = 0) -> dict:
    arg_keys = jax.random.split(jax.random.key(seed), 7)
    return {
        "grad_out": centred(arg_keys[0], (SEQS, CHANNELS, SEQ_LEN), 1.0, 6.0, ((0, 2), (1, 4), (2, 4)), jnp.float32),
        "query": centred(arg_keys[1], (SEQS, CHANNELS, SEQ_LEN), 1.0, 6.0, ((0, 2), (1, 4), (2, 4)), jnp.float32),
        "keys": centred(arg_keys[2], (SEQS, CHANNELS, SEQ_LEN), 1.0, 6.0, ((0, 2), (1, 4), (2, 4)), jnp.float32),
        "values": centred(arg_keys[3], (SEQS, CHANNELS, SEQ_LEN), 1.0, 6.0, ((0, 2), (1, 4), (2, 4)), jnp.float32),
        "long_filter": centred(arg_keys[4], (CHANNELS, SEQ_LEN), 1.0, 6.0, ((0, 16),), jnp.float32),
        "short_filter": centred(arg_keys[5], (CHANNELS, TAPS), TAPS ** -0.5, 3.5, ((0, 4),), jnp.float32),
    }


def depthwise(signal, kernel):
    return lax.conv_general_dilated(signal, kernel[:, None, :], (1,), "VALID", dimension_numbers=("NCH", "OIH", "NCH"), feature_group_count=kernel.shape[0], precision=lax.Precision.HIGHEST)


def reference(grad_out, query, keys, values, long_filter, short_filter):
    padded_len = 2 * SEQ_LEN
    scale_factor = SEQ_LEN ** -0.5
    key_window = jnp.pad(keys, ((0, 0), (0, 0), (TAPS - 1, 0)))
    short_keys = depthwise(key_window, jnp.flip(short_filter, 1))
    gated = short_keys * values
    grad_conv = grad_out * query
    spec_gated = jnp.fft.rfft(gated, padded_len, axis=2)
    spec_filter = jnp.fft.rfft(long_filter, padded_len, axis=1)[None]
    spec_grad = jnp.fft.rfft(grad_conv, padded_len, axis=2)
    conv_out = jnp.fft.irfft(spec_gated * spec_filter, padded_len, axis=2)[:, :, :SEQ_LEN] * scale_factor
    grad_gated = jnp.fft.irfft(spec_grad * jnp.conj(spec_filter), padded_len, axis=2)[:, :, :SEQ_LEN] * scale_factor
    cross_spec = jnp.sum(spec_grad * jnp.conj(spec_gated), axis=0)
    grad_long = jnp.fft.irfft(cross_spec, padded_len, axis=1)[:, :SEQ_LEN] * scale_factor
    grad_query = grad_out * conv_out
    grad_short = grad_gated * values
    grad_values = grad_gated * short_keys
    grad_window = jnp.pad(grad_short, ((0, 0), (0, 0), (0, TAPS - 1)))
    grad_keys = depthwise(grad_window, short_filter)
    return grad_query, grad_keys, grad_values, grad_long
```

```python
import functools
import math

import jax
import jax.numpy as jnp
import numpy as np
from jax import lax
from jax.experimental import pallas as pl
from jax.experimental.pallas import tpu as pltpu
from jax.sharding import PartitionSpec as P

LANES = 128
SUBLANES = 8
MESH = pl.DeviceIdType.MESH


def plan(length):
    padded = 2 * length
    inner = LANES
    while inner * inner < 4 * padded:
        inner *= 2
    return padded, padded // inner, inner


def split_bf16(table):
    high = table.astype(jnp.bfloat16)
    low = (table - high.astype(np.float64)).astype(jnp.bfloat16)
    return high, low


def make_tables(length):
    padded, outer, inner = plan(length)
    ids = np.arange(inner)
    phase = 2.0 * math.pi / inner * (ids[:, None] * ids[None, :] % inner)
    cos, sin = np.cos(phase), np.sin(phase)
    forward = np.block([[cos, -sin], [sin, cos]])
    backward = np.block([[cos, sin], [-sin, cos]]) / padded * length ** (-0.5)
    turn = 2.0 * math.pi / padded * (np.arange(outer // 2 + 1)[:, None] * ids[None, :])
    turns = np.stack([np.cos(turn), np.sin(turn)])[:, :, None, :]
    turns = np.broadcast_to(turns, (2, outer // 2 + 1, SUBLANES, inner)).astype(np.float32)
    return (*split_bf16(forward), *split_bf16(backward), turns)


def half_fft(x):
    n = len(x)
    if n == 1:
        return [(x[0], None), (x[0], None)]
    even, odd = half_fft(x[0::2]), half_fft(x[1::2])
    bins = [None] * (n + 1)
    bins[0] = (even[0][0] + odd[0][0], None)
    bins[n] = (even[0][0] - odd[0][0], None)
    bins[n // 2] = (even[n // 2][0], -odd[n // 2][0])
    for k in range(1, n // 2):
        c, s = math.cos(math.pi * k / n), math.sin(math.pi * k / n)
        (er, ei), (orr, oi) = even[k], odd[k]
        tr = orr * c + oi * s
        ti = oi * c - orr * s
        bins[k] = (er + tr, ei + ti)
        bins[n - k] = (er - tr, ti - ei)
    return bins


def half_ifft(bins):
    n = len(bins) - 1
    if n == 1:
        return [bins[0][0] + bins[1][0]]
    even, odd = [None] * (n // 2 + 1), [None] * (n // 2 + 1)
    even[0] = (bins[0][0] + bins[n][0], None)
    odd[0] = (bins[0][0] - bins[n][0], None)
    even[n // 2] = (2.0 * bins[n // 2][0], None)
    odd[n // 2] = (-2.0 * bins[n // 2][1], None)
    for k in range(1, n // 2):
        c, s = math.cos(math.pi * k / n), math.sin(math.pi * k / n)
        (ar, ai), (br, bi) = bins[k], bins[n - k]
        even[k] = (ar + br, ai - bi)
        dr, di = ar - br, ai + bi
        odd[k] = (dr * c - di * s, dr * s + di * c)
    out = [None] * n
    out[0::2] = half_ifft(even)
    out[1::2] = half_ifft(odd)
    return out


def kernel(
    ctx,
    seqs,
    go_ref,
    q_ref,
    k_ref,
    v_ref,
    lf_ref,
    sf_ref,
    fh_ref,
    fl_ref,
    bh_ref,
    bl_ref,
    turn_ref,
    gq_ref,
    gk_ref,
    gv_ref,
    gl_ref,
    d_src,
    g_src,
    sk_ref,
    gs_ref,
    d_own,
    g_own,
    gg_src,
    cv_src,
    gg_back,
    cv_back,
    cross,
    cross_in,
    spec_h,
    spec_d,
    spec_g,
    work,
    halo,
    send_sems,
    recv_sems,
    cross_send,
    cross_recv,
    halo_send,
    halo_recv,
):
    me = lax.axis_index("ctx")
    my_seq = lax.axis_index("seq")
    chans, tok = k_ref.shape
    own = chans // ctx
    taps = sf_ref.shape[1]
    length = tok * ctx
    _, outer, inner = plan(length)
    bins = outer // 2 + 1
    chunk = work.shape[1]
    chunks = own // chunk
    per_tok = tok // inner

    def peer(off):
        return lax.rem(me + off, ctx)

    barrier = pltpu.get_barrier_semaphore()
    for off in range(1, ctx):
        pl.semaphore_signal(barrier, inc=1, device_id={"ctx": peer(off)}, device_id_type=MESH)
    for off in range(1, seqs):
        pl.semaphore_signal(
            barrier,
            inc=1,
            device_id={"seq": lax.rem(my_seq + off, seqs)},
            device_id_type=MESH,
        )
    d_src[...] = go_ref[...] * q_ref[...]
    halo[0] = k_ref[:, tok - LANES :].T[LANES - SUBLANES :, :]
    pl.semaphore_wait(barrier, ctx - 1 + seqs - 1)

    def halo_copy(which, off):
        return pltpu.make_async_remote_copy(
            src_ref=halo.at[2 * which],
            dst_ref=halo.at[2 * which + 1],
            send_sem=halo_send.at[which],
            recv_sem=halo_recv.at[which],
            device_id={"ctx": peer(off)},
            device_id_type=MESH,
        )

    def block(start, size):
        return pl.ds(pl.multiple_of(start, SUBLANES), size)

    def out_copy(kind, src, dst, off, c):
        return pltpu.make_async_remote_copy(
            src_ref=src.at[block(peer(off) * own + c * chunk, chunk)],
            dst_ref=dst.at[me, pl.ds(c * chunk, chunk)],
            send_sem=send_sems.at[kind, off, c],
            recv_sem=recv_sems.at[kind, off, c],
            device_id={"ctx": peer(off)},
            device_id_type=MESH,
        )

    def back_copy(kind, src, dst, off, c):
        return pltpu.make_async_remote_copy(
            src_ref=src.at[peer(off), pl.ds(c * chunk, chunk)],
            dst_ref=dst.at[block(me * own + c * chunk, chunk)],
            send_sem=send_sems.at[kind, off, c],
            recv_sem=recv_sems.at[kind, off, c],
            device_id={"ctx": peer(off)},
            device_id_type=MESH,
        )

    def cross_copy(off, c):
        return pltpu.make_async_remote_copy(
            src_ref=cross.at[pl.ds(0, ctx), pl.ds(c * chunk, chunk)],
            dst_ref=cross_in.at[off - 1, pl.ds(0, ctx), pl.ds(c * chunk, chunk)],
            send_sem=cross_send.at[off, c],
            recv_sem=cross_recv.at[off, c],
            device_id={"seq": lax.rem(my_seq + off, seqs)},
            device_id_type=MESH,
        )

    started = []

    def start(copy):
        copy.start()
        started.append(copy)
        return copy

    key_halo = start(halo_copy(0, 1))
    d_copies = {}
    for c in range(chunks):
        for off in range(ctx - 1, 0, -1):
            d_copies[off, c] = start(out_copy(0, d_src, d_own, off, c))
    d_own[me] = d_src[block(me * own, own)]

    key_halo.wait_recv()
    before = jnp.concatenate([halo[1]] * (LANES // SUBLANES), axis=0).T
    before = jnp.where(me > 0, before, 0.0)
    for z in range(ctx):
        rows = slice(z * own, (z + 1) * own)
        window = jnp.concatenate([before[rows], k_ref[rows, :]], axis=1)
        total = k_ref[rows, :] * sf_ref[rows, 0:1]
        for j in range(1, taps):
            total = total + pltpu.roll(window, j, 1)[:, LANES:] * sf_ref[rows, j : j + 1]
        sk_ref[rows, :] = total
        g_src[rows, :] = total * v_ref[rows, :]
    g_copies = {}
    for c in range(chunks):
        for off in range(ctx - 1, 0, -1):
            g_copies[off, c] = start(out_copy(1, g_src, g_own, off, c))
    g_own[me] = g_src[block(me * own, own)]

    def multiply(high_ref, low_ref):
        x = work[...].reshape(bins * chunk, 2 * inner)
        high = x.astype(jnp.bfloat16)
        low = (x - high.astype(jnp.float32)).astype(jnp.bfloat16)
        dot = functools.partial(jnp.dot, preferred_element_type=jnp.float32)
        y = dot(high, high_ref[...]) + dot(low, high_ref[...]) + dot(high, low_ref[...])
        return y.reshape(bins, chunk, 2 * inner)

    def transform(load, c, spec):
        def rows_step(i, carry):
            base = c * chunk + i * SUBLANES
            for lane in range(0, inner, LANES):
                x = [load(t, base, lane) for t in range(outer // 2)]
                for k, (re, im) in enumerate(half_fft(x)):
                    if k == 0:
                        re, im = re, jnp.zeros_like(re)
                    else:
                        cos = turn_ref[0, k, :, lane : lane + LANES]
                        sin = turn_ref[1, k, :, lane : lane + LANES]
                        if im is None:
                            re, im = re * cos, -re * sin
                        else:
                            re, im = re * cos + im * sin, im * cos - re * sin
                    at = block(i * SUBLANES, SUBLANES)
                    work[k, at, lane : lane + LANES] = re
                    work[k, at, inner + lane : inner + lane + LANES] = im
            return carry

        lax.fori_loop(0, chunk // SUBLANES, rows_step, 0)
        spec[:, c * chunk : (c + 1) * chunk, :] = multiply(fh_ref, fl_ref)

    def load_from(ref):
        def load(t, base, lane):
            at = (t % per_tok) * inner + lane
            return ref[t // per_tok, block(base, SUBLANES), at : at + LANES]

        return load

    def load_filter(t, base, lane):
        at = t * inner + lane
        return lf_ref[block(base, SUBLANES), at : at + LANES]

    def product(a, b, c, conjugate):
        rows = slice(c * chunk, (c + 1) * chunk)

        def step(k, carry):
            ar, ai = a[k, rows, :inner], a[k, rows, inner:]
            br, bi = b[k, rows, :inner], b[k, rows, inner:]
            if conjugate:
                work[k, :, :inner] = ar * br + ai * bi
                work[k, :, inner:] = ai * br - ar * bi
            else:
                work[k, :, :inner] = ar * br - ai * bi
                work[k, :, inner:] = ar * bi + ai * br
            return carry

        lax.fori_loop(0, bins, step, 0)

    def inverse(c, dst):
        work[...] = multiply(bh_ref, bl_ref)

        def rows_step(i, carry):
            at = block(i * SUBLANES, SUBLANES)
            for lane in range(0, inner, LANES):
                z = []
                for k in range(bins):
                    re = work[k, at, lane : lane + LANES]
                    if k == 0:
                        z.append((re, None))
                        continue
                    im = work[k, at, inner + lane : inner + lane + LANES]
                    cos = turn_ref[0, k, :, lane : lane + LANES]
                    sin = turn_ref[1, k, :, lane : lane + LANES]
                    z.append((re * cos - im * sin, re * sin + im * cos))
                for t, x in enumerate(half_ifft(z)):
                    col = (t % per_tok) * inner + lane
                    dst[t // per_tok, block(c * chunk + i * SUBLANES, SUBLANES), col : col + LANES] = x
            return carry

        lax.fori_loop(0, chunk // SUBLANES, rows_step, 0)

    def keep_own(c, src, dst):
        dst[block(me * own + c * chunk, chunk)] = src[me, pl.ds(c * chunk, chunk)]

    for c in range(chunks):
        transform(load_filter, c, spec_h)

    gg_copies, cv_copies, cross_copies = {}, {}, {}
    for c in range(chunks):
        for off in range(1, ctx):
            d_copies[off, c].wait_recv()
        transform(load_from(d_own), c, spec_d)
        product(spec_d, spec_h, c, True)
        inverse(c, gg_src)
        for off in range(ctx - 1, 0, -1):
            gg_copies[off, c] = start(back_copy(2, gg_src, gg_back, off, c))
        keep_own(c, gg_src, gg_back)
    for c in range(chunks):
        for off in range(1, ctx):
            g_copies[off, c].wait_recv()
        transform(load_from(g_own), c, spec_g)
        product(spec_g, spec_h, c, False)
        inverse(c, cv_src)
        for off in range(ctx - 1, 0, -1):
            cv_copies[off, c] = start(back_copy(3, cv_src, cv_back, off, c))
        product(spec_d, spec_g, c, True)
        inverse(c, cross)
        for off in range(1, seqs):
            cross_copies[off, c] = start(cross_copy(off, c))
        keep_own(c, cv_src, cv_back)

    for copy in gg_copies.values():
        copy.wait_recv()
    grad_gated = gg_back[...]
    gs_ref[...] = grad_gated * v_ref[...]
    halo[2] = gs_ref[:, :LANES].T[:SUBLANES, :]
    head_halo = start(halo_copy(1, ctx - 1))
    gv_ref[...] = gg_back[...] * sk_ref[...]
    head_halo.wait_recv()
    after = jnp.concatenate([halo[3]] * (LANES // SUBLANES), axis=0).T
    after = jnp.where(me < ctx - 1, after, 0.0)
    for z in range(ctx):
        rows = slice(z * own, (z + 1) * own)
        window = jnp.concatenate([gs_ref[rows, :], after[rows]], axis=1)
        total = gs_ref[rows, :] * sf_ref[rows, 0:1]
        for j in range(1, taps):
            total = total + pltpu.roll(window, tok + LANES - j, 1)[:, :tok] * sf_ref[rows, j : j + 1]
        gk_ref[rows, :] = total

    for (off, c), copy in cv_copies.items():
        copy.wait_recv()
    gq_ref[...] = go_ref[...] * cv_back[...]

    for copy in cross_copies.values():
        copy.wait_recv()
    for z in range(ctx):
        total = cross[z]
        for off in range(1, seqs):
            total = total + cross_in[off - 1, z]
        gl_ref[:, z * tok : (z + 1) * tok] = total
    for copy in started:
        copy.wait_send()


def shards(ctx, seqs, grad_out, query, keys, values, long_filter, short_filter):
    chans, tok = keys.shape[1:]
    own = chans // ctx
    length = tok * ctx
    _, outer, inner = plan(length)
    bins = outer // 2 + 1
    chunk = math.gcd(own, 16)
    chunks = own // chunk
    tables = make_tables(length)
    f32 = jnp.float32
    tokens = jax.ShapeDtypeStruct((chans, tok), f32)
    vmem = pl.BlockSpec(memory_space=pltpu.VMEM)
    position = pltpu.VMEM((chans, tok), f32)
    channel = pltpu.VMEM((ctx, own, tok), f32)
    spectrum = pltpu.VMEM((bins, own, 2 * inner), f32)
    dma = pltpu.SemaphoreType.DMA
    operands = [x.reshape(chans, tok) for x in (grad_out, query, keys, values)]
    operands += [long_filter, short_filter, *(jnp.asarray(t) for t in tables)]
    outs = pl.pallas_call(
        functools.partial(kernel, ctx, seqs),
        out_shape=(tokens, tokens, tokens, jax.ShapeDtypeStruct((own, length), f32)),
        in_specs=[vmem] * len(operands),
        out_specs=(vmem,) * 4,
        scratch_shapes=[
            position,
            position,
            position,
            position,
            channel,
            channel,
            channel,
            channel,
            position,
            position,
            channel,
            pltpu.VMEM((max(seqs - 1, 1), ctx, own, tok), f32),
            spectrum,
            spectrum,
            spectrum,
            pltpu.VMEM((bins, chunk, 2 * inner), f32),
            pltpu.VMEM((4, SUBLANES, chans), f32),
            dma((4, ctx, chunks)),
            dma((4, ctx, chunks)),
            dma((seqs, chunks)),
            dma((seqs, chunks)),
            dma((2,)),
            dma((2,)),
        ],
        compiler_params=pltpu.CompilerParams(
            collective_id=0, has_side_effects=True, vmem_limit_bytes=48 * 1024 * 1024
        ),
    )(*operands)
    gq, gk, gv, gl = outs
    return (gq[None], gk[None], gv[None], gl)


def solution(mesh):
    tokens = P("seq", "ch", "ctx")
    return jax.shard_map(
        functools.partial(shards, mesh.shape["ctx"], mesh.shape["seq"]),
        mesh=mesh,
        in_specs=(tokens, tokens, tokens, tokens, P(("ch", "ctx"), None), P("ch", None)),
        out_specs=(tokens, tokens, tokens, P(("ch", "ctx"), None)),
        check_vma=False,
    )
```

```python
import functools
import math

import jax
import jax.numpy as jnp
import numpy as np
from jax import lax
from jax.experimental import pallas as pl
from jax.experimental.pallas import tpu as pltpu
from jax.sharding import PartitionSpec as P

LANES = 128
VMEM_BYTES = 62 * 1024 * 1024
SUBLANES = 8
MESH = pl.DeviceIdType.MESH


def plan(length):
    padded = 2 * length
    inner = LANES
    while inner * inner < 4 * padded:
        inner *= 2
    return padded, padded // inner, inner


def make_tables(length):
    padded, outer, inner = plan(length)
    ids = np.arange(inner)
    phase = 2.0 * math.pi / inner * (ids[:, None] * ids[None, :] % inner)
    cos, sin = np.cos(phase), np.sin(phase)
    forward = np.block([[cos, -sin], [sin, cos]])
    backward = np.block([[cos, sin], [-sin, cos]]) / padded * length ** (-0.5)
    turn = 2.0 * math.pi / padded * (np.arange(outer // 2 + 1)[:, None] * ids[None, :])
    turns = np.stack([np.cos(turn), np.sin(turn)])[:, :, None, :]
    turns = np.broadcast_to(turns, (2, outer // 2 + 1, SUBLANES, inner)).astype(np.float32)
    products = np.concatenate([forward, backward]).astype(np.float32)
    return products, turns


def half_fft(x):
    n = len(x)
    if n == 1:
        return [(x[0], None), (x[0], None)]
    even, odd = half_fft(x[0::2]), half_fft(x[1::2])
    bins = [None] * (n + 1)
    bins[0] = (even[0][0] + odd[0][0], None)
    bins[n] = (even[0][0] - odd[0][0], None)
    bins[n // 2] = (even[n // 2][0], -odd[n // 2][0])
    for k in range(1, n // 2):
        c, s = math.cos(math.pi * k / n), math.sin(math.pi * k / n)
        (er, ei), (orr, oi) = even[k], odd[k]
        tr = orr * c + oi * s
        ti = oi * c - orr * s
        bins[k] = (er + tr, ei + ti)
        bins[n - k] = (er - tr, ti - ei)
    return bins


def half_ifft(bins):
    n = len(bins) - 1
    if n == 1:
        return [bins[0][0] + bins[1][0]]
    even, odd = [None] * (n // 2 + 1), [None] * (n // 2 + 1)
    even[0] = (bins[0][0] + bins[n][0], None)
    odd[0] = (bins[0][0] - bins[n][0], None)
    even[n // 2] = (2.0 * bins[n // 2][0], None)
    odd[n // 2] = (-2.0 * bins[n // 2][1], None)
    for k in range(1, n // 2):
        c, s = math.cos(math.pi * k / n), math.sin(math.pi * k / n)
        (ar, ai), (br, bi) = bins[k], bins[n - k]
        even[k] = (ar + br, ai - bi)
        dr, di = ar - br, ai + bi
        odd[k] = (dr * c - di * s, dr * s + di * c)
    out = [None] * n
    out[0::2] = half_ifft(even)
    out[1::2] = half_ifft(odd)
    return out


def kernel(
    ctx,
    seqs,
    go_hbm,
    q_hbm,
    k_hbm,
    v_hbm,
    lf_hbm,
    sf_hbm,
    table_hbm,
    turn_hbm,
    gq_ref,
    gk_ref,
    gv_ref,
    gl_ref,
    go_ref,
    q_ref,
    k_ref,
    v_ref,
    lf_ref,
    sf_ref,
    table_ref,
    turn_ref,
    load_sems,
    table_split,
    taps_ref,
    d_src,
    g_src,
    sk_ref,
    gs_ref,
    d_own,
    g_own,
    gg_src,
    cv_src,
    gg_back,
    cv_back,
    cross,
    cross_in,
    spec_h,
    spec_d,
    spec_g,
    work,
    halo,
    send_sems,
    recv_sems,
    cross_send,
    cross_recv,
    halo_send,
    halo_recv,
):
    me = lax.axis_index("ctx")
    my_seq = lax.axis_index("seq")
    chans, tok = k_ref.shape
    own = chans // ctx
    taps = sf_ref.shape[0]
    length = tok * ctx
    _, outer, inner = plan(length)
    bins = outer // 2 + 1
    chunk = work.shape[1]
    chunks = own // chunk
    per_tok = tok // inner

    def peer(off):
        return lax.rem(me + off, ctx)

    barrier = pltpu.get_barrier_semaphore()
    for off in range(1, ctx):
        pl.semaphore_signal(barrier, inc=1, device_id={"ctx": peer(off)}, device_id_type=MESH)
    for off in range(1, seqs):
        pl.semaphore_signal(
            barrier,
            inc=1,
            device_id={"seq": lax.rem(my_seq + off, seqs)},
            device_id_type=MESH,
        )
    pairs = (
        (go_hbm, go_ref),
        (q_hbm, q_ref),
        (k_hbm, k_ref),
        (sf_hbm, sf_ref),
        (v_hbm, v_ref),
        (lf_hbm, lf_ref),
        (turn_hbm, turn_ref),
        (table_hbm, table_ref),
    )
    loads = [
        pltpu.make_async_copy(src, dst, load_sems.at[i]) for i, (src, dst) in enumerate(pairs)
    ]
    for load in loads:
        load.start()
    go_load, q_load, k_load, sf_load, v_load, lf_load, turn_load, table_load = loads
    go_load.wait()
    q_load.wait()
    d_src[...] = go_ref[...] * q_ref[...]
    k_load.wait()
    halo[0] = k_ref[:, tok - LANES :].T[LANES - SUBLANES :, :]
    pl.semaphore_wait(barrier, ctx - 1 + seqs - 1)

    def halo_copy(which, off):
        return pltpu.make_async_remote_copy(
            src_ref=halo.at[2 * which],
            dst_ref=halo.at[2 * which + 1],
            send_sem=halo_send.at[which],
            recv_sem=halo_recv.at[which],
            device_id={"ctx": peer(off)},
            device_id_type=MESH,
        )

    def block(start, size):
        return pl.ds(pl.multiple_of(start, SUBLANES), size)

    def out_copy(kind, src, dst, off, c):
        return pltpu.make_async_remote_copy(
            src_ref=src.at[block(peer(off) * own + c * chunk, chunk)],
            dst_ref=dst.at[me, pl.ds(c * chunk, chunk)],
            send_sem=send_sems.at[kind, off, c],
            recv_sem=recv_sems.at[kind, off, c],
            device_id={"ctx": peer(off)},
            device_id_type=MESH,
        )

    def back_copy(kind, src, dst, off, c):
        return pltpu.make_async_remote_copy(
            src_ref=src.at[peer(off), pl.ds(c * chunk, chunk)],
            dst_ref=dst.at[block(me * own + c * chunk, chunk)],
            send_sem=send_sems.at[kind, off, c],
            recv_sem=recv_sems.at[kind, off, c],
            device_id={"ctx": peer(off)},
            device_id_type=MESH,
        )

    def cross_copy(off, c):
        return pltpu.make_async_remote_copy(
            src_ref=cross.at[pl.ds(0, ctx), pl.ds(c * chunk, chunk)],
            dst_ref=cross_in.at[off - 1, pl.ds(0, ctx), pl.ds(c * chunk, chunk)],
            send_sem=cross_send.at[off, c],
            recv_sem=cross_recv.at[off, c],
            device_id={"seq": lax.rem(my_seq + off, seqs)},
            device_id_type=MESH,
        )

    started = []

    def start(copy):
        copy.start()
        started.append(copy)
        return copy

    key_halo = start(halo_copy(0, 1))
    d_copies = {}
    for c in range(chunks):
        for off in range(ctx - 1, 0, -1):
            d_copies[off, c] = start(out_copy(0, d_src, d_own, off, c))
    d_own[me] = d_src[block(me * own, own)]

    sf_load.wait()
    for j in range(taps):
        taps_ref[j] = jnp.broadcast_to(sf_ref[j : j + 1, :], (LANES, chans)).T

    def tap(j, rows):
        return jnp.concatenate([taps_ref[j, rows, :]] * (tok // LANES), axis=1)

    v_load.wait()
    key_halo.wait_recv()
    before = jnp.concatenate([halo[1]] * (LANES // SUBLANES), axis=0).T
    before = jnp.where(me > 0, before, 0.0)
    for z in range(ctx):
        rows = slice(z * own, (z + 1) * own)
        window = jnp.concatenate([before[rows], k_ref[rows, :]], axis=1)
        total = k_ref[rows, :] * tap(0, rows)
        for j in range(1, taps):
            total = total + pltpu.roll(window, j, 1)[:, LANES:] * tap(j, rows)
        sk_ref[rows, :] = total
        g_src[rows, :] = total * v_ref[rows, :]
    g_copies = {}
    for c in range(chunks):
        for off in range(ctx - 1, 0, -1):
            g_copies[off, c] = start(out_copy(1, g_src, g_own, off, c))
    g_own[me] = g_src[block(me * own, own)]

    def split(x):
        high = x.astype(jnp.bfloat16)
        return high, (x - high.astype(jnp.float32)).astype(jnp.bfloat16)

    def table(i):
        return table_split[i]

    def multiply(first):
        x = work[...].reshape(bins * chunk, 2 * inner)
        high, low = split(x)
        dot = functools.partial(jnp.dot, preferred_element_type=jnp.float32)
        y = dot(high, table(first)) + dot(low, table(first)) + dot(high, table(first + 1))
        return y.reshape(bins, chunk, 2 * inner)

    def transform(load, c, spec):
        def rows_step(i, carry):
            base = c * chunk + i * SUBLANES
            for lane in range(0, inner, LANES):
                x = [load(t, base, lane) for t in range(outer // 2)]
                for k, (re, im) in enumerate(half_fft(x)):
                    if k == 0:
                        re, im = re, jnp.zeros_like(re)
                    else:
                        cos = turn_ref[0, k, :, lane : lane + LANES]
                        sin = turn_ref[1, k, :, lane : lane + LANES]
                        if im is None:
                            re, im = re * cos, -re * sin
                        else:
                            re, im = re * cos + im * sin, im * cos - re * sin
                    at = block(i * SUBLANES, SUBLANES)
                    work[k, at, lane : lane + LANES] = re
                    work[k, at, inner + lane : inner + lane + LANES] = im
            return carry

        lax.fori_loop(0, chunk // SUBLANES, rows_step, 0)
        spec[:, c * chunk : (c + 1) * chunk, :] = multiply(0)

    def load_from(ref):
        def load(t, base, lane):
            at = (t % per_tok) * inner + lane
            return ref[t // per_tok, block(base, SUBLANES), at : at + LANES]

        return load

    def load_filter(t, base, lane):
        at = t * inner + lane
        return lf_ref[block(base, SUBLANES), at : at + LANES]

    def product(a, b, c, conjugate):
        rows = slice(c * chunk, (c + 1) * chunk)

        def step(k, carry):
            ar, ai = a[k, rows, :inner], a[k, rows, inner:]
            br, bi = b[k, rows, :inner], b[k, rows, inner:]
            if conjugate:
                work[k, :, :inner] = ar * br + ai * bi
                work[k, :, inner:] = ai * br - ar * bi
            else:
                work[k, :, :inner] = ar * br - ai * bi
                work[k, :, inner:] = ar * bi + ai * br
            return carry

        lax.fori_loop(0, bins, step, 0)

    def inverse(c, dst):
        work[...] = multiply(2)

        def rows_step(i, carry):
            at = block(i * SUBLANES, SUBLANES)
            for lane in range(0, inner, LANES):
                z = []
                for k in range(bins):
                    re = work[k, at, lane : lane + LANES]
                    if k == 0:
                        z.append((re, None))
                        continue
                    im = work[k, at, inner + lane : inner + lane + LANES]
                    cos = turn_ref[0, k, :, lane : lane + LANES]
                    sin = turn_ref[1, k, :, lane : lane + LANES]
                    z.append((re * cos - im * sin, re * sin + im * cos))
                for t, x in enumerate(half_ifft(z)):
                    col = (t % per_tok) * inner + lane
                    dst[t // per_tok, block(c * chunk + i * SUBLANES, SUBLANES), col : col + LANES] = x
            return carry

        lax.fori_loop(0, chunk // SUBLANES, rows_step, 0)

    def keep_own(c, src, dst):
        dst[block(me * own + c * chunk, chunk)] = src[me, pl.ds(c * chunk, chunk)]

    lf_load.wait()
    turn_load.wait()
    table_load.wait()
    for i in range(2):
        whole = table_ref[i * 2 * inner : (i + 1) * 2 * inner, :]
        table_split[2 * i], table_split[2 * i + 1] = split(whole)
    for c in range(chunks):
        transform(load_filter, c, spec_h)

    gg_copies, cv_copies, cross_copies = {}, {}, {}
    for c in range(chunks):
        for off in range(1, ctx):
            d_copies[off, c].wait_recv()
        transform(load_from(d_own), c, spec_d)
        product(spec_d, spec_h, c, True)
        inverse(c, gg_src)
        for off in range(ctx - 1, 0, -1):
            gg_copies[off, c] = start(back_copy(2, gg_src, gg_back, off, c))
        keep_own(c, gg_src, gg_back)
    for c in range(chunks):
        for off in range(1, ctx):
            g_copies[off, c].wait_recv()
        transform(load_from(g_own), c, spec_g)
        product(spec_g, spec_h, c, False)
        inverse(c, cv_src)
        for off in range(ctx - 1, 0, -1):
            cv_copies[off, c] = start(back_copy(3, cv_src, cv_back, off, c))
        product(spec_d, spec_g, c, True)
        inverse(c, cross)
        for off in range(1, seqs):
            cross_copies[off, c] = start(cross_copy(off, c))
        keep_own(c, cv_src, cv_back)

    for copy in gg_copies.values():
        copy.wait_recv()
    grad_gated = gg_back[...]
    gs_ref[...] = grad_gated * v_ref[...]
    halo[2] = gs_ref[:, :LANES].T[:SUBLANES, :]
    head_halo = start(halo_copy(1, ctx - 1))
    gv_ref[...] = gg_back[...] * sk_ref[...]
    head_halo.wait_recv()
    after = jnp.concatenate([halo[3]] * (LANES // SUBLANES), axis=0).T
    after = jnp.where(me < ctx - 1, after, 0.0)
    for z in range(ctx):
        rows = slice(z * own, (z + 1) * own)
        window = jnp.concatenate([gs_ref[rows, :], after[rows]], axis=1)
        total = gs_ref[rows, :] * tap(0, rows)
        for j in range(1, taps):
            total = total + pltpu.roll(window, tok + LANES - j, 1)[:, :tok] * tap(j, rows)
        gk_ref[rows, :] = total

    for (off, c), copy in cv_copies.items():
        copy.wait_recv()
    gq_ref[...] = go_ref[...] * cv_back[...]

    for copy in cross_copies.values():
        copy.wait_recv()
    for z in range(ctx):
        total = cross[z]
        for off in range(1, seqs):
            total = total + cross_in[off - 1, z]
        gl_ref[:, z * tok : (z + 1) * tok] = total
    for copy in started:
        copy.wait_send()


def store(*refs):
    count = (len(refs) - 1) // 2
    copies = [
        pltpu.make_async_copy(refs[i], refs[count + i], refs[-1].at[i]) for i in range(count)
    ]
    for copy in copies:
        copy.start()
    for copy in copies:
        copy.wait()


def shards(ctx, seqs, grad_out, query, keys, values, long_filter, short_filter):
    chans, tok = keys.shape[1:]
    own = chans // ctx
    length = tok * ctx
    _, outer, inner = plan(length)
    bins = outer // 2 + 1
    chunk = math.gcd(own, 16)
    chunks = own // chunk
    tables = make_tables(length)
    f32 = jnp.float32
    tokens = jax.ShapeDtypeStruct((chans, tok), f32)
    vmem = pl.BlockSpec(memory_space=pltpu.VMEM)
    position = pltpu.VMEM((chans, tok), f32)
    channel = pltpu.VMEM((ctx, own, tok), f32)
    spectrum = pltpu.VMEM((bins, own, 2 * inner), f32)
    dma = pltpu.SemaphoreType.DMA
    operands = [x.reshape(chans, tok) for x in (grad_out, query, keys, values)]
    operands += [long_filter, short_filter.T, *(jnp.asarray(t) for t in tables)]
    hbm = pl.BlockSpec(memory_space=pltpu.HBM)
    outs = pl.pallas_call(
        functools.partial(kernel, ctx, seqs),
        out_shape=(tokens, tokens, tokens, jax.ShapeDtypeStruct((own, length), f32)),
        in_specs=[hbm] * len(operands),
        out_specs=(vmem,) * 4,
        scratch_shapes=[
            *(pltpu.VMEM(operands[i].shape, operands[i].dtype) for i in range(len(operands))),
            dma((len(operands),)),
            pltpu.VMEM((4, 2 * inner, 2 * inner), jnp.bfloat16),
            pltpu.VMEM((short_filter.shape[1], chans, LANES), f32),
            position,
            position,
            position,
            position,
            channel,
            channel,
            channel,
            channel,
            position,
            position,
            channel,
            pltpu.VMEM((max(seqs - 1, 1), ctx, own, tok), f32),
            spectrum,
            spectrum,
            spectrum,
            pltpu.VMEM((bins, chunk, 2 * inner), f32),
            pltpu.VMEM((4, SUBLANES, chans), f32),
            dma((4, ctx, chunks)),
            dma((4, ctx, chunks)),
            dma((seqs, chunks)),
            dma((seqs, chunks)),
            dma((2,)),
            dma((2,)),
        ],
        compiler_params=pltpu.CompilerParams(
            collective_id=0, has_side_effects=True, vmem_limit_bytes=VMEM_BYTES
        ),
    )(*operands)
    gq, gk, gv, gl = pl.pallas_call(
        store,
        out_shape=tuple(jax.ShapeDtypeStruct(x.shape, f32) for x in outs),
        in_specs=[hbm] * 4,
        out_specs=(hbm,) * 4,
        scratch_shapes=[dma((4,))],
        compiler_params=pltpu.CompilerParams(vmem_limit_bytes=VMEM_BYTES),
    )(*outs)
    return (gq[None], gk[None], gv[None], gl)


def solution(mesh):
    tokens = P("seq", "ch", "ctx")
    return jax.shard_map(
        functools.partial(shards, mesh.shape["ctx"], mesh.shape["seq"]),
        mesh=mesh,
        in_specs=(tokens, tokens, tokens, tokens, P(("ch", "ctx"), None), P("ch", None)),
        out_specs=(tokens, tokens, tokens, P(("ch", "ctx"), None)),
        check_vma=False,
    )
```

```python
import functools
import math

import jax
import jax.numpy as jnp
import numpy as np
from jax import lax
from jax.experimental import pallas as pl
from jax.experimental.pallas import tpu as pltpu
from jax.sharding import PartitionSpec as P

LANES = 128
VMEM_BYTES = 62 * 1024 * 1024
SUBLANES = 8
MESH = pl.DeviceIdType.MESH


def plan(length):
    padded = 2 * length
    inner = LANES
    while inner * inner < 4 * padded:
        inner *= 2
    return padded, padded // inner, inner


def make_tables(length):
    padded, outer, inner = plan(length)
    ids = np.arange(inner)
    phase = 2.0 * math.pi / inner * (ids[:, None] * ids[None, :] % inner)
    cos, sin = np.cos(phase), np.sin(phase)
    forward = np.block([[cos, -sin], [sin, cos]])
    backward = np.block([[cos, sin], [-sin, cos]]) / padded * length ** (-0.5)
    turn = 2.0 * math.pi / padded * (np.arange(outer // 2 + 1)[:, None] * ids[None, :])
    turns = np.stack([np.cos(turn), np.sin(turn)])[:, :, None, :]
    turns = np.broadcast_to(turns, (2, outer // 2 + 1, SUBLANES, inner)).astype(np.float32)
    products = np.concatenate([forward, backward]).astype(np.float32)
    return products, turns


def half_fft(x):
    n = len(x)
    if n == 1:
        return [(x[0], None), (x[0], None)]
    even, odd = half_fft(x[0::2]), half_fft(x[1::2])
    bins = [None] * (n + 1)
    bins[0] = (even[0][0] + odd[0][0], None)
    bins[n] = (even[0][0] - odd[0][0], None)
    bins[n // 2] = (even[n // 2][0], -odd[n // 2][0])
    for k in range(1, n // 2):
        c, s = math.cos(math.pi * k / n), math.sin(math.pi * k / n)
        (er, ei), (orr, oi) = even[k], odd[k]
        tr = orr * c + oi * s
        ti = oi * c - orr * s
        bins[k] = (er + tr, ei + ti)
        bins[n - k] = (er - tr, ti - ei)
    return bins


def half_ifft(bins):
    n = len(bins) - 1
    if n == 1:
        return [bins[0][0] + bins[1][0]]
    even, odd = [None] * (n // 2 + 1), [None] * (n // 2 + 1)
    even[0] = (bins[0][0] + bins[n][0], None)
    odd[0] = (bins[0][0] - bins[n][0], None)
    even[n // 2] = (2.0 * bins[n // 2][0], None)
    odd[n // 2] = (-2.0 * bins[n // 2][1], None)
    for k in range(1, n // 2):
        c, s = math.cos(math.pi * k / n), math.sin(math.pi * k / n)
        (ar, ai), (br, bi) = bins[k], bins[n - k]
        even[k] = (ar + br, ai - bi)
        dr, di = ar - br, ai + bi
        odd[k] = (dr * c - di * s, dr * s + di * c)
    out = [None] * n
    out[0::2] = half_ifft(even)
    out[1::2] = half_ifft(odd)
    return out


def kernel(
    ctx,
    seqs,
    go_hbm,
    q_hbm,
    k_hbm,
    v_hbm,
    lf_hbm,
    sf_hbm,
    table_hbm,
    turn_hbm,
    gk_hbm,
    gv_hbm,
    cv_back,
    part_hbm,
    cross_in,
    gk_ref,
    gv_ref,
    go_ref,
    q_ref,
    k_ref,
    v_ref,
    lf_ref,
    sf_ref,
    table_ref,
    turn_ref,
    load_sems,
    table_split,
    taps_ref,
    d_src,
    g_src,
    sk_ref,
    gs_ref,
    d_own,
    g_own,
    gg_src,
    cv_src,
    gg_back,
    cross,
    spec_h,
    spec_d,
    spec_g,
    work,
    halo,
    send_sems,
    recv_sems,
    cross_send,
    cross_recv,
    halo_send,
    halo_recv,
    store_sems,
    keep_sems,
):
    me = lax.axis_index("ctx")
    my_seq = lax.axis_index("seq")
    chans, tok = k_ref.shape
    own = chans // ctx
    taps = sf_ref.shape[0]
    length = tok * ctx
    _, outer, inner = plan(length)
    bins = outer // 2 + 1
    chunk = work.shape[1]
    chunks = own // chunk
    per_tok = tok // inner

    def peer(off):
        return lax.rem(me + off, ctx)

    barrier = pltpu.get_barrier_semaphore()
    for off in range(1, ctx):
        pl.semaphore_signal(barrier, inc=1, device_id={"ctx": peer(off)}, device_id_type=MESH)
    for off in range(1, seqs):
        pl.semaphore_signal(
            barrier,
            inc=1,
            device_id={"seq": lax.rem(my_seq + off, seqs)},
            device_id_type=MESH,
        )
    pairs = (
        (go_hbm, go_ref),
        (q_hbm, q_ref),
        (k_hbm, k_ref),
        (sf_hbm, sf_ref),
        (v_hbm, v_ref),
        (lf_hbm, lf_ref),
        (turn_hbm, turn_ref),
        (table_hbm, table_ref),
    )
    loads = [
        pltpu.make_async_copy(src, dst, load_sems.at[i]) for i, (src, dst) in enumerate(pairs)
    ]
    for load in loads:
        load.start()
    go_load, q_load, k_load, sf_load, v_load, lf_load, turn_load, table_load = loads
    go_load.wait()
    q_load.wait()
    d_src[...] = go_ref[...] * q_ref[...]
    k_load.wait()
    halo[0] = k_ref[:, tok - LANES :].T[LANES - SUBLANES :, :]
    pl.semaphore_wait(barrier, ctx - 1 + seqs - 1)

    def halo_copy(which, off):
        return pltpu.make_async_remote_copy(
            src_ref=halo.at[2 * which],
            dst_ref=halo.at[2 * which + 1],
            send_sem=halo_send.at[which],
            recv_sem=halo_recv.at[which],
            device_id={"ctx": peer(off)},
            device_id_type=MESH,
        )

    def block(start, size):
        return pl.ds(pl.multiple_of(start, SUBLANES), size)

    def out_copy(kind, src, dst, off, c):
        return pltpu.make_async_remote_copy(
            src_ref=src.at[block(peer(off) * own + c * chunk, chunk)],
            dst_ref=dst.at[me, pl.ds(c * chunk, chunk)],
            send_sem=send_sems.at[kind, off, c],
            recv_sem=recv_sems.at[kind, off, c],
            device_id={"ctx": peer(off)},
            device_id_type=MESH,
        )

    def back_copy(kind, src, dst, off, c):
        return pltpu.make_async_remote_copy(
            src_ref=src.at[peer(off), pl.ds(c * chunk, chunk)],
            dst_ref=dst.at[block(me * own + c * chunk, chunk)],
            send_sem=send_sems.at[kind, off, c],
            recv_sem=recv_sems.at[kind, off, c],
            device_id={"ctx": peer(off)},
            device_id_type=MESH,
        )

    def cross_copy(off, c):
        return pltpu.make_async_remote_copy(
            src_ref=cross.at[pl.ds(0, ctx), pl.ds(c * chunk, chunk)],
            dst_ref=cross_in.at[off - 1, pl.ds(0, ctx), pl.ds(c * chunk, chunk)],
            send_sem=cross_send.at[off, c],
            recv_sem=cross_recv.at[off, c],
            device_id={"seq": lax.rem(my_seq + off, seqs)},
            device_id_type=MESH,
        )

    started = []

    def start(copy):
        copy.start()
        started.append(copy)
        return copy

    key_halo = start(halo_copy(0, 1))
    d_copies = {}
    for c in range(chunks):
        for off in range(ctx - 1, 0, -1):
            d_copies[off, c] = start(out_copy(0, d_src, d_own, off, c))
    d_own[me] = d_src[block(me * own, own)]

    sf_load.wait()
    for j in range(taps):
        taps_ref[j] = jnp.broadcast_to(sf_ref[j : j + 1, :], (LANES, chans)).T

    def tap(j, rows):
        return jnp.concatenate([taps_ref[j, rows, :]] * (tok // LANES), axis=1)

    v_load.wait()
    key_halo.wait_recv()
    before = jnp.concatenate([halo[1]] * (LANES // SUBLANES), axis=0).T
    before = jnp.where(me > 0, before, 0.0)
    for z in range(ctx):
        rows = slice(z * own, (z + 1) * own)
        window = jnp.concatenate([before[rows], k_ref[rows, :]], axis=1)
        total = k_ref[rows, :] * tap(0, rows)
        for j in range(1, taps):
            total = total + pltpu.roll(window, j, 1)[:, LANES:] * tap(j, rows)
        sk_ref[rows, :] = total
        g_src[rows, :] = total * v_ref[rows, :]
    g_copies = {}
    for c in range(chunks):
        for off in range(ctx - 1, 0, -1):
            g_copies[off, c] = start(out_copy(1, g_src, g_own, off, c))
    g_own[me] = g_src[block(me * own, own)]

    def split(x):
        high = x.astype(jnp.bfloat16)
        return high, (x - high.astype(jnp.float32)).astype(jnp.bfloat16)

    def table(i):
        return table_split[i]

    def multiply(first):
        x = work[...].reshape(bins * chunk, 2 * inner)
        high, low = split(x)
        dot = functools.partial(jnp.dot, preferred_element_type=jnp.float32)
        y = dot(high, table(first)) + dot(low, table(first)) + dot(high, table(first + 1))
        return y.reshape(bins, chunk, 2 * inner)

    def transform(load, c, spec):
        def rows_step(i, carry):
            base = c * chunk + i * SUBLANES
            for lane in range(0, inner, LANES):
                x = [load(t, base, lane) for t in range(outer // 2)]
                for k, (re, im) in enumerate(half_fft(x)):
                    if k == 0:
                        re, im = re, jnp.zeros_like(re)
                    else:
                        cos = turn_ref[0, k, :, lane : lane + LANES]
                        sin = turn_ref[1, k, :, lane : lane + LANES]
                        if im is None:
                            re, im = re * cos, -re * sin
                        else:
                            re, im = re * cos + im * sin, im * cos - re * sin
                    at = block(i * SUBLANES, SUBLANES)
                    work[k, at, lane : lane + LANES] = re
                    work[k, at, inner + lane : inner + lane + LANES] = im
            return carry

        lax.fori_loop(0, chunk // SUBLANES, rows_step, 0)
        spec[:, c * chunk : (c + 1) * chunk, :] = multiply(0)

    def load_from(ref):
        def load(t, base, lane):
            at = (t % per_tok) * inner + lane
            return ref[t // per_tok, block(base, SUBLANES), at : at + LANES]

        return load

    def load_filter(t, base, lane):
        at = t * inner + lane
        return lf_ref[block(base, SUBLANES), at : at + LANES]

    def product(a, b, c, conjugate):
        rows = slice(c * chunk, (c + 1) * chunk)

        def step(k, carry):
            ar, ai = a[k, rows, :inner], a[k, rows, inner:]
            br, bi = b[k, rows, :inner], b[k, rows, inner:]
            if conjugate:
                work[k, :, :inner] = ar * br + ai * bi
                work[k, :, inner:] = ai * br - ar * bi
            else:
                work[k, :, :inner] = ar * br - ai * bi
                work[k, :, inner:] = ar * bi + ai * br
            return carry

        lax.fori_loop(0, bins, step, 0)

    def inverse(c, dst):
        work[...] = multiply(2)

        def rows_step(i, carry):
            at = block(i * SUBLANES, SUBLANES)
            for lane in range(0, inner, LANES):
                z = []
                for k in range(bins):
                    re = work[k, at, lane : lane + LANES]
                    if k == 0:
                        z.append((re, None))
                        continue
                    im = work[k, at, inner + lane : inner + lane + LANES]
                    cos = turn_ref[0, k, :, lane : lane + LANES]
                    sin = turn_ref[1, k, :, lane : lane + LANES]
                    z.append((re * cos - im * sin, re * sin + im * cos))
                for t, x in enumerate(half_ifft(z)):
                    col = (t % per_tok) * inner + lane
                    dst[t // per_tok, block(c * chunk + i * SUBLANES, SUBLANES), col : col + LANES] = x
            return carry

        lax.fori_loop(0, chunk // SUBLANES, rows_step, 0)

    def own_rows(c):
        return block(me * own + c * chunk, chunk)

    def chunk_rows(c):
        return pl.ds(c * chunk, chunk)

    stores = []

    def store(src, dst, sem):
        copy = pltpu.make_async_copy(src, dst, sem)
        copy.start()
        stores.append(copy)

    lf_load.wait()
    turn_load.wait()
    table_load.wait()
    for i in range(2):
        whole = table_ref[i * 2 * inner : (i + 1) * 2 * inner, :]
        table_split[2 * i], table_split[2 * i + 1] = split(whole)
    for c in range(chunks):
        transform(load_filter, c, spec_h)

    gg_copies, cv_copies, cross_copies = {}, {}, {}
    for c in range(chunks):
        for off in range(1, ctx):
            d_copies[off, c].wait_recv()
        transform(load_from(d_own), c, spec_d)
        product(spec_d, spec_h, c, True)
        inverse(c, gg_src)
        for off in range(ctx - 1, 0, -1):
            gg_copies[off, c] = start(back_copy(2, gg_src, gg_back, off, c))
        gg_back[own_rows(c)] = gg_src[me, chunk_rows(c)]
    for c in range(chunks):
        for off in range(1, ctx):
            g_copies[off, c].wait_recv()
        transform(load_from(g_own), c, spec_g)
        product(spec_g, spec_h, c, False)
        inverse(c, cv_src)
        for off in range(ctx - 1, 0, -1):
            cv_copies[off, c] = start(back_copy(3, cv_src, cv_back, off, c))
        product(spec_d, spec_g, c, True)
        inverse(c, cross)
        for off in range(1, seqs):
            cross_copies[off, c] = start(cross_copy(off, c))
        store(cv_src.at[me, chunk_rows(c)], cv_back.at[own_rows(c)], keep_sems.at[0, c])
        store(
            cross.at[pl.ds(0, ctx), chunk_rows(c)],
            part_hbm.at[pl.ds(0, ctx), chunk_rows(c)],
            keep_sems.at[1, c],
        )

    for copy in gg_copies.values():
        copy.wait_recv()
    grad_gated = gg_back[...]
    gs_ref[...] = grad_gated * v_ref[...]
    halo[2] = gs_ref[:, :LANES].T[:SUBLANES, :]
    head_halo = start(halo_copy(1, ctx - 1))
    gv_ref[...] = gg_back[...] * sk_ref[...]
    store(gv_ref, gv_hbm, store_sems.at[0])
    head_halo.wait_recv()
    after = jnp.concatenate([halo[3]] * (LANES // SUBLANES), axis=0).T
    after = jnp.where(me < ctx - 1, after, 0.0)
    for z in range(ctx):
        rows = slice(z * own, (z + 1) * own)
        window = jnp.concatenate([gs_ref[rows, :], after[rows]], axis=1)
        total = gs_ref[rows, :] * tap(0, rows)
        for j in range(1, taps):
            total = total + pltpu.roll(window, tok + LANES - j, 1)[:, :tok] * tap(j, rows)
        gk_ref[rows, :] = total

    store(gk_ref, gk_hbm, store_sems.at[1])

    for copy in (*cv_copies.values(), *cross_copies.values()):
        copy.wait_recv()
    for copy in stores:
        copy.wait()
    for copy in started:
        copy.wait_send()


def finish(
    gk_hbm,
    gv_hbm,
    go_hbm,
    cv_hbm,
    part_hbm,
    cross_hbm,
    gq_out,
    gk_out,
    gv_out,
    gl_out,
    gk_ref,
    gv_ref,
    go_ref,
    cv_ref,
    part_ref,
    cross_ref,
    gl_ref,
    load_sems,
    store_sems,
):
    pairs = (
        (gk_hbm, gk_ref),
        (gv_hbm, gv_ref),
        (go_hbm, go_ref),
        (cv_hbm, cv_ref),
        (part_hbm, part_ref),
        (cross_hbm, cross_ref),
    )
    loads = [
        pltpu.make_async_copy(src, dst, load_sems.at[i]) for i, (src, dst) in enumerate(pairs)
    ]
    for load in loads:
        load.start()
    stores = []

    def store(src, dst):
        copy = pltpu.make_async_copy(src, dst, store_sems.at[len(stores)])
        copy.start()
        stores.append(copy)

    loads[0].wait()
    store(gk_ref, gk_out)
    loads[1].wait()
    store(gv_ref, gv_out)
    loads[2].wait()
    loads[3].wait()
    cv_ref[...] = cv_ref[...] * go_ref[...]
    store(cv_ref, gq_out)
    loads[4].wait()
    loads[5].wait()
    ctx, _, tok = part_ref.shape
    for z in range(ctx):
        total = part_ref[z]
        for other in range(cross_ref.shape[0]):
            total = total + cross_ref[other, z]
        gl_ref[:, z * tok : (z + 1) * tok] = total
    store(gl_ref, gl_out)
    for copy in stores:
        copy.wait()


def shards(ctx, seqs, grad_out, query, keys, values, long_filter, short_filter):
    chans, tok = keys.shape[1:]
    own = chans // ctx
    length = tok * ctx
    _, outer, inner = plan(length)
    bins = outer // 2 + 1
    chunk = math.gcd(own, 16)
    chunks = own // chunk
    tables = make_tables(length)
    f32 = jnp.float32
    tokens = jax.ShapeDtypeStruct((chans, tok), f32)
    position = pltpu.VMEM((chans, tok), f32)
    channel = pltpu.VMEM((ctx, own, tok), f32)
    spectrum = pltpu.VMEM((bins, own, 2 * inner), f32)
    dma = pltpu.SemaphoreType.DMA
    operands = [x.reshape(chans, tok) for x in (grad_out, query, keys, values)]
    operands += [long_filter, short_filter.T, *(jnp.asarray(t) for t in tables)]
    hbm = pl.BlockSpec(memory_space=pltpu.HBM)
    outs = pl.pallas_call(
        functools.partial(kernel, ctx, seqs),
        out_shape=(
            tokens,
            tokens,
            tokens,
            jax.ShapeDtypeStruct((ctx, own, tok), f32),
            jax.ShapeDtypeStruct((max(seqs - 1, 1), ctx, own, tok), f32),
        ),
        in_specs=[hbm] * len(operands),
        out_specs=(hbm,) * 5,
        scratch_shapes=[
            position,
            position,
            *(pltpu.VMEM(operands[i].shape, operands[i].dtype) for i in range(len(operands))),
            dma((len(operands),)),
            pltpu.VMEM((4, 2 * inner, 2 * inner), jnp.bfloat16),
            pltpu.VMEM((short_filter.shape[1], chans, LANES), f32),
            position,
            position,
            position,
            position,
            channel,
            channel,
            channel,
            channel,
            position,
            channel,
            spectrum,
            spectrum,
            spectrum,
            pltpu.VMEM((bins, chunk, 2 * inner), f32),
            pltpu.VMEM((4, SUBLANES, chans), f32),
            dma((4, ctx, chunks)),
            dma((4, ctx, chunks)),
            dma((seqs, chunks)),
            dma((seqs, chunks)),
            dma((2,)),
            dma((2,)),
            dma((2,)),
            dma((2, chunks)),
        ],
        compiler_params=pltpu.CompilerParams(
            collective_id=0, has_side_effects=True, vmem_limit_bytes=VMEM_BYTES
        ),
    )(*operands)
    gk, gv, cv, part, cross = outs
    operands = [gk, gv, operands[0], cv, part, cross]
    result = jax.ShapeDtypeStruct((own, length), f32)
    gq, gk, gv, gl = pl.pallas_call(
        finish,
        out_shape=(tokens, tokens, tokens, result),
        in_specs=[hbm] * len(operands),
        out_specs=(hbm,) * 4,
        scratch_shapes=[
            *(pltpu.VMEM(x.shape, f32) for x in operands),
            pltpu.VMEM(result.shape, f32),
            dma((len(operands),)),
            dma((4,)),
        ],
        compiler_params=pltpu.CompilerParams(vmem_limit_bytes=VMEM_BYTES),
    )(*operands)
    return (gq[None], gk[None], gv[None], gl)


def solution(mesh):
    tokens = P("seq", "ch", "ctx")
    return jax.shard_map(
        functools.partial(shards, mesh.shape["ctx"], mesh.shape["seq"]),
        mesh=mesh,
        in_specs=(tokens, tokens, tokens, tokens, P(("ch", "ctx"), None), P("ch", None)),
        out_specs=(tokens, tokens, tokens, P(("ch", "ctx"), None)),
        check_vma=False,
    )
```

```python
import functools
import math

import jax
import jax.numpy as jnp
import numpy as np
from jax import lax
from jax.experimental import pallas as pl
from jax.experimental.pallas import tpu as pltpu
from jax.sharding import PartitionSpec as P

LANES = 128
VMEM_BYTES = 62 * 1024 * 1024
SUBLANES = 8
MESH = pl.DeviceIdType.MESH


def plan(length):
    padded = 2 * length
    inner = LANES
    while inner * inner < 4 * padded:
        inner *= 2
    return padded, padded // inner, inner


def make_tables(length):
    padded, outer, inner = plan(length)
    ids = np.arange(inner)
    phase = 2.0 * math.pi / inner * (ids[:, None] * ids[None, :] % inner)
    cos, sin = np.cos(phase), np.sin(phase)
    forward = np.block([[cos, -sin], [sin, cos]])
    backward = np.block([[cos, sin], [-sin, cos]]) / padded * length ** (-0.5)
    turn = 2.0 * math.pi / padded * (np.arange(outer // 2 + 1)[:, None] * ids[None, :])
    turns = np.stack([np.cos(turn), np.sin(turn)])[:, :, None, :]
    turns = np.broadcast_to(turns, (2, outer // 2 + 1, SUBLANES, inner)).astype(np.float32)
    products = np.concatenate([forward, backward]).astype(np.float32)
    return products, turns


def half_fft(x):
    n = len(x)
    if n == 1:
        return [(x[0], None), (x[0], None)]
    even, odd = half_fft(x[0::2]), half_fft(x[1::2])
    bins = [None] * (n + 1)
    bins[0] = (even[0][0] + odd[0][0], None)
    bins[n] = (even[0][0] - odd[0][0], None)
    bins[n // 2] = (even[n // 2][0], -odd[n // 2][0])
    for k in range(1, n // 2):
        c, s = math.cos(math.pi * k / n), math.sin(math.pi * k / n)
        (er, ei), (orr, oi) = even[k], odd[k]
        tr = orr * c + oi * s
        ti = oi * c - orr * s
        bins[k] = (er + tr, ei + ti)
        bins[n - k] = (er - tr, ti - ei)
    return bins


def half_ifft(bins):
    n = len(bins) - 1
    if n == 1:
        return [bins[0][0] + bins[1][0]]
    even, odd = [None] * (n // 2 + 1), [None] * (n // 2 + 1)
    even[0] = (bins[0][0] + bins[n][0], None)
    odd[0] = (bins[0][0] - bins[n][0], None)
    even[n // 2] = (2.0 * bins[n // 2][0], None)
    odd[n // 2] = (-2.0 * bins[n // 2][1], None)
    for k in range(1, n // 2):
        c, s = math.cos(math.pi * k / n), math.sin(math.pi * k / n)
        (ar, ai), (br, bi) = bins[k], bins[n - k]
        even[k] = (ar + br, ai - bi)
        dr, di = ar - br, ai + bi
        odd[k] = (dr * c - di * s, dr * s + di * c)
    out = [None] * n
    out[0::2] = half_ifft(even)
    out[1::2] = half_ifft(odd)
    return out


def kernel(
    ctx,
    seqs,
    go_hbm,
    q_hbm,
    k_hbm,
    v_hbm,
    lf_hbm,
    sf_hbm,
    table_hbm,
    turn_hbm,
    gk_hbm,
    gv_hbm,
    cv_back,
    part_hbm,
    cross_in,
    gk_ref,
    gv_ref,
    go_ref,
    q_ref,
    k_ref,
    v_ref,
    lf_ref,
    sf_ref,
    table_ref,
    turn_ref,
    load_sems,
    table_split,
    taps_ref,
    d_src,
    g_src,
    sk_ref,
    gs_ref,
    d_own,
    g_own,
    gg_src,
    cv_src,
    gg_back,
    cross,
    spec_h,
    spec_d,
    spec_g,
    work,
    halo,
    send_sems,
    recv_sems,
    cross_send,
    cross_recv,
    halo_send,
    halo_recv,
    store_sems,
    keep_sems,
):
    me = lax.axis_index("ctx")
    my_seq = lax.axis_index("seq")
    chans, tok = k_ref.shape
    own = chans // ctx
    taps = sf_ref.shape[0]
    length = tok * ctx
    _, outer, inner = plan(length)
    bins = outer // 2 + 1
    chunk = work.shape[1]
    chunks = own // chunk
    per_tok = tok // inner

    def peer(off):
        return lax.rem(me + off, ctx)

    barrier = pltpu.get_barrier_semaphore()
    for off in range(1, ctx):
        pl.semaphore_signal(barrier, inc=1, device_id={"ctx": peer(off)}, device_id_type=MESH)
    for off in range(1, seqs):
        pl.semaphore_signal(
            barrier,
            inc=1,
            device_id={"seq": lax.rem(my_seq + off, seqs)},
            device_id_type=MESH,
        )
    pairs = (
        (go_hbm, go_ref),
        (q_hbm, q_ref),
        (k_hbm, k_ref),
        (sf_hbm, sf_ref),
        (v_hbm, v_ref),
        (lf_hbm, lf_ref),
        (turn_hbm, turn_ref),
        (table_hbm, table_ref),
    )
    loads = [
        pltpu.make_async_copy(src, dst, load_sems.at[i]) for i, (src, dst) in enumerate(pairs)
    ]
    for load in loads:
        load.start()
    go_load, q_load, k_load, sf_load, v_load, lf_load, turn_load, table_load = loads
    go_load.wait()
    q_load.wait()
    d_src[...] = go_ref[...] * q_ref[...]
    k_load.wait()
    halo[0] = k_ref[:, tok - LANES :].T[LANES - SUBLANES :, :]
    pl.semaphore_wait(barrier, ctx - 1 + seqs - 1)

    def halo_copy(which, off):
        return pltpu.make_async_remote_copy(
            src_ref=halo.at[2 * which],
            dst_ref=halo.at[2 * which + 1],
            send_sem=halo_send.at[which],
            recv_sem=halo_recv.at[which],
            device_id={"ctx": peer(off)},
            device_id_type=MESH,
        )

    def block(start, size):
        return pl.ds(pl.multiple_of(start, SUBLANES), size)

    def out_copy(kind, src, dst, off, c):
        return pltpu.make_async_remote_copy(
            src_ref=src.at[block(peer(off) * own + c * chunk, chunk)],
            dst_ref=dst.at[me, pl.ds(c * chunk, chunk)],
            send_sem=send_sems.at[kind, off, c],
            recv_sem=recv_sems.at[kind, off, c],
            device_id={"ctx": peer(off)},
            device_id_type=MESH,
        )

    def back_copy(kind, src, dst, off, c):
        return pltpu.make_async_remote_copy(
            src_ref=src.at[peer(off), pl.ds(c * chunk, chunk)],
            dst_ref=dst.at[block(me * own + c * chunk, chunk)],
            send_sem=send_sems.at[kind, off, c],
            recv_sem=recv_sems.at[kind, off, c],
            device_id={"ctx": peer(off)},
            device_id_type=MESH,
        )

    def cross_copy(off, c):
        return pltpu.make_async_remote_copy(
            src_ref=cross.at[pl.ds(0, ctx), pl.ds(c * chunk, chunk)],
            dst_ref=cross_in.at[off - 1, pl.ds(0, ctx), pl.ds(c * chunk, chunk)],
            send_sem=cross_send.at[off, c],
            recv_sem=cross_recv.at[off, c],
            device_id={"seq": lax.rem(my_seq + off, seqs)},
            device_id_type=MESH,
        )

    started = []

    def start(copy):
        copy.start()
        started.append(copy)
        return copy

    key_halo = start(halo_copy(0, 1))
    d_copies = {}
    for c in range(chunks):
        for off in range(ctx - 1, 0, -1):
            d_copies[off, c] = start(out_copy(0, d_src, d_own, off, c))
    d_own[me] = d_src[block(me * own, own)]

    sf_load.wait()
    for j in range(taps):
        taps_ref[j] = jnp.broadcast_to(sf_ref[j : j + 1, :], (LANES, chans)).T

    def tap(j, rows):
        return jnp.concatenate([taps_ref[j, rows, :]] * (tok // LANES), axis=1)

    v_load.wait()
    key_halo.wait_recv()
    before = jnp.concatenate([halo[1]] * (LANES // SUBLANES), axis=0).T
    before = jnp.where(me > 0, before, 0.0)
    for z in range(ctx):
        rows = slice(z * own, (z + 1) * own)
        window = jnp.concatenate([before[rows], k_ref[rows, :]], axis=1)
        total = k_ref[rows, :] * tap(0, rows)
        for j in range(1, taps):
            total = total + pltpu.roll(window, j, 1)[:, LANES:] * tap(j, rows)
        sk_ref[rows, :] = total
        g_src[rows, :] = total * v_ref[rows, :]
    g_copies = {}
    for c in range(chunks):
        for off in range(ctx - 1, 0, -1):
            g_copies[off, c] = start(out_copy(1, g_src, g_own, off, c))
    g_own[me] = g_src[block(me * own, own)]

    def split(x):
        high = x.astype(jnp.bfloat16)
        return high, (x - high.astype(jnp.float32)).astype(jnp.bfloat16)

    def table(i):
        return table_split[i]

    def multiply(first):
        x = work[...].reshape(bins * chunk, 2 * inner)
        high, low = split(x)
        dot = functools.partial(jnp.dot, preferred_element_type=jnp.float32)
        y = dot(high, table(first)) + dot(low, table(first)) + dot(high, table(first + 1))
        return y.reshape(bins, chunk, 2 * inner)

    def transform(load, c, spec):
        def rows_step(i, carry):
            base = c * chunk + i * SUBLANES
            for lane in range(0, inner, LANES):
                x = [load(t, base, lane) for t in range(outer // 2)]
                for k, (re, im) in enumerate(half_fft(x)):
                    if k == 0:
                        re, im = re, jnp.zeros_like(re)
                    else:
                        cos = turn_ref[0, k, :, lane : lane + LANES]
                        sin = turn_ref[1, k, :, lane : lane + LANES]
                        if im is None:
                            re, im = re * cos, -re * sin
                        else:
                            re, im = re * cos + im * sin, im * cos - re * sin
                    at = block(i * SUBLANES, SUBLANES)
                    work[k, at, lane : lane + LANES] = re
                    work[k, at, inner + lane : inner + lane + LANES] = im
            return carry

        lax.fori_loop(0, chunk // SUBLANES, rows_step, 0)
        spec[:, c * chunk : (c + 1) * chunk, :] = multiply(0)

    def load_from(ref):
        def load(t, base, lane):
            at = (t % per_tok) * inner + lane
            return ref[t // per_tok, block(base, SUBLANES), at : at + LANES]

        return load

    def load_filter(t, base, lane):
        at = t * inner + lane
        return lf_ref[block(base, SUBLANES), at : at + LANES]

    def product(a, b, c, conjugate):
        rows = slice(c * chunk, (c + 1) * chunk)

        def step(k, carry):
            ar, ai = a[k, rows, :inner], a[k, rows, inner:]
            br, bi = b[k, rows, :inner], b[k, rows, inner:]
            if conjugate:
                work[k, :, :inner] = ar * br + ai * bi
                work[k, :, inner:] = ai * br - ar * bi
            else:
                work[k, :, :inner] = ar * br - ai * bi
                work[k, :, inner:] = ar * bi + ai * br
            return carry

        lax.fori_loop(0, bins, step, 0)

    def inverse(c, dst):
        work[...] = multiply(2)

        def rows_step(i, carry):
            at = block(i * SUBLANES, SUBLANES)
            for lane in range(0, inner, LANES):
                z = []
                for k in range(bins):
                    re = work[k, at, lane : lane + LANES]
                    if k == 0:
                        z.append((re, None))
                        continue
                    im = work[k, at, inner + lane : inner + lane + LANES]
                    cos = turn_ref[0, k, :, lane : lane + LANES]
                    sin = turn_ref[1, k, :, lane : lane + LANES]
                    z.append((re * cos - im * sin, re * sin + im * cos))
                for t, x in enumerate(half_ifft(z)):
                    col = (t % per_tok) * inner + lane
                    dst[t // per_tok, block(c * chunk + i * SUBLANES, SUBLANES), col : col + LANES] = x
            return carry

        lax.fori_loop(0, chunk // SUBLANES, rows_step, 0)

    def own_rows(c):
        return block(me * own + c * chunk, chunk)

    def chunk_rows(c):
        return pl.ds(c * chunk, chunk)

    stores = []

    def store(src, dst, sem):
        copy = pltpu.make_async_copy(src, dst, sem)
        copy.start()
        stores.append(copy)

    lf_load.wait()
    turn_load.wait()
    table_load.wait()
    for i in range(2):
        whole = table_ref[i * 2 * inner : (i + 1) * 2 * inner, :]
        table_split[2 * i], table_split[2 * i + 1] = split(whole)
    for c in range(chunks):
        transform(load_filter, c, spec_h)

    gg_copies, cv_copies, cross_copies = {}, {}, {}
    for c in range(chunks):
        for off in range(1, ctx):
            d_copies[off, c].wait_recv()
        transform(load_from(d_own), c, spec_d)
        product(spec_d, spec_h, c, True)
        inverse(c, gg_src)
        for off in range(ctx - 1, 0, -1):
            gg_copies[off, c] = start(back_copy(2, gg_src, gg_back, off, c))
        gg_back[own_rows(c)] = gg_src[me, chunk_rows(c)]
    for c in range(chunks):
        for off in range(1, ctx):
            g_copies[off, c].wait_recv()
        transform(load_from(g_own), c, spec_g)
        product(spec_g, spec_h, c, False)
        inverse(c, cv_src)
        for off in range(ctx - 1, 0, -1):
            cv_copies[off, c] = start(back_copy(3, cv_src, cv_back, off, c))
        product(spec_d, spec_g, c, True)
        inverse(c, cross)
        for off in range(1, seqs):
            cross_copies[off, c] = start(cross_copy(off, c))
        store(cv_src.at[me, chunk_rows(c)], cv_back.at[own_rows(c)], keep_sems.at[0, c])
        store(
            cross.at[pl.ds(0, ctx), chunk_rows(c)],
            part_hbm.at[pl.ds(0, ctx), chunk_rows(c)],
            keep_sems.at[1, c],
        )

    for copy in gg_copies.values():
        copy.wait_recv()
    grad_gated = gg_back[...]
    gs_ref[...] = grad_gated * v_ref[...]
    halo[2] = gs_ref[:, :LANES].T[:SUBLANES, :]
    head_halo = start(halo_copy(1, ctx - 1))
    gv_ref[...] = gg_back[...] * sk_ref[...]
    store(gv_ref, gv_hbm, store_sems.at[0])
    head_halo.wait_recv()
    after = jnp.concatenate([halo[3]] * (LANES // SUBLANES), axis=0).T
    after = jnp.where(me < ctx - 1, after, 0.0)
    for z in range(ctx):
        rows = slice(z * own, (z + 1) * own)
        window = jnp.concatenate([gs_ref[rows, :], after[rows]], axis=1)
        total = gs_ref[rows, :] * tap(0, rows)
        for j in range(1, taps):
            total = total + pltpu.roll(window, tok + LANES - j, 1)[:, :tok] * tap(j, rows)
        gk_ref[rows, :] = total

    store(gk_ref, gk_hbm, store_sems.at[1])

    for copy in (*cv_copies.values(), *cross_copies.values()):
        copy.wait_recv()
    for copy in stores:
        copy.wait()
    for copy in started:
        copy.wait_send()


def finish(
    gk_hbm,
    gv_hbm,
    go_hbm,
    cv_hbm,
    part_hbm,
    cross_hbm,
    gq_out,
    gk_out,
    gv_out,
    gl_out,
    gk_ref,
    gv_ref,
    go_ref,
    cv_ref,
    part_ref,
    cross_ref,
    gl_ref,
    load_sems,
    store_sems,
):
    pairs = (
        (gk_hbm, gk_ref),
        (gv_hbm, gv_ref),
        (go_hbm, go_ref),
        (cv_hbm, cv_ref),
        (part_hbm, part_ref),
        (cross_hbm, cross_ref),
    )
    loads = [
        pltpu.make_async_copy(src, dst, load_sems.at[i]) for i, (src, dst) in enumerate(pairs)
    ]
    for load in loads:
        load.start()
    stores = []

    def store(src, dst):
        copy = pltpu.make_async_copy(src, dst, store_sems.at[len(stores)])
        copy.start()
        stores.append(copy)

    loads[0].wait()
    store(gk_ref, gk_out)
    loads[1].wait()
    store(gv_ref, gv_out)
    loads[2].wait()
    loads[3].wait()
    cv_ref[...] = cv_ref[...] * go_ref[...]
    store(cv_ref, gq_out)
    loads[4].wait()
    loads[5].wait()
    ctx, _, tok = part_ref.shape
    for z in range(ctx):
        total = part_ref[z]
        for other in range(cross_ref.shape[0]):
            total = total + cross_ref[other, z]
        gl_ref[:, z * tok : (z + 1) * tok] = total
    store(gl_ref, gl_out)
    for copy in stores:
        copy.wait()


def shards(ctx, seqs, grad_out, query, keys, values, long_filter, short_filter):
    chans, tok = keys.shape[1:]
    own = chans // ctx
    length = tok * ctx
    _, outer, inner = plan(length)
    bins = outer // 2 + 1
    chunk = math.gcd(own, 8)
    chunks = own // chunk
    tables = make_tables(length)
    f32 = jnp.float32
    tokens = jax.ShapeDtypeStruct((chans, tok), f32)
    position = pltpu.VMEM((chans, tok), f32)
    channel = pltpu.VMEM((ctx, own, tok), f32)
    spectrum = pltpu.VMEM((bins, own, 2 * inner), f32)
    dma = pltpu.SemaphoreType.DMA
    operands = [x.reshape(chans, tok) for x in (grad_out, query, keys, values)]
    operands += [long_filter, short_filter.T, *(jnp.asarray(t) for t in tables)]
    hbm = pl.BlockSpec(memory_space=pltpu.HBM)
    outs = pl.pallas_call(
        functools.partial(kernel, ctx, seqs),
        out_shape=(
            tokens,
            tokens,
            tokens,
            jax.ShapeDtypeStruct((ctx, own, tok), f32),
            jax.ShapeDtypeStruct((max(seqs - 1, 1), ctx, own, tok), f32),
        ),
        in_specs=[hbm] * len(operands),
        out_specs=(hbm,) * 5,
        scratch_shapes=[
            position,
            position,
            *(pltpu.VMEM(operands[i].shape, operands[i].dtype) for i in range(len(operands))),
            dma((len(operands),)),
            pltpu.VMEM((4, 2 * inner, 2 * inner), jnp.bfloat16),
            pltpu.VMEM((short_filter.shape[1], chans, LANES), f32),
            position,
            position,
            position,
            position,
            channel,
            channel,
            channel,
            channel,
            position,
            channel,
            spectrum,
            spectrum,
            spectrum,
            pltpu.VMEM((bins, chunk, 2 * inner), f32),
            pltpu.VMEM((4, SUBLANES, chans), f32),
            dma((4, ctx, chunks)),
            dma((4, ctx, chunks)),
            dma((seqs, chunks)),
            dma((seqs, chunks)),
            dma((2,)),
            dma((2,)),
            dma((2,)),
            dma((2, chunks)),
        ],
        compiler_params=pltpu.CompilerParams(
            collective_id=0, has_side_effects=True, vmem_limit_bytes=VMEM_BYTES
        ),
    )(*operands)
    gk, gv, cv, part, cross = outs
    operands = [gk, gv, operands[0], cv, part, cross]
    result = jax.ShapeDtypeStruct((own, length), f32)
    gq, gk, gv, gl = pl.pallas_call(
        finish,
        out_shape=(tokens, tokens, tokens, result),
        in_specs=[hbm] * len(operands),
        out_specs=(hbm,) * 4,
        scratch_shapes=[
            *(pltpu.VMEM(x.shape, f32) for x in operands),
            pltpu.VMEM(result.shape, f32),
            dma((len(operands),)),
            dma((4,)),
        ],
        compiler_params=pltpu.CompilerParams(vmem_limit_bytes=VMEM_BYTES),
    )(*operands)
    return (gq[None], gk[None], gv[None], gl)


def solution(mesh):
    tokens = P("seq", "ch", "ctx")
    return jax.shard_map(
        functools.partial(shards, mesh.shape["ctx"], mesh.shape["seq"]),
        mesh=mesh,
        in_specs=(tokens, tokens, tokens, tokens, P(("ch", "ctx"), None), P("ch", None)),
        out_specs=(tokens, tokens, tokens, P(("ch", "ctx"), None)),
        check_vma=False,
    )
```

```python
import functools
import math

import jax
import jax.numpy as jnp
import numpy as np
from jax import lax
from jax.experimental import pallas as pl
from jax.experimental.pallas import tpu as pltpu
from jax.sharding import PartitionSpec as P

LANES = 128
VMEM_BYTES = 62 * 1024 * 1024
SUBLANES = 8
MESH = pl.DeviceIdType.MESH


def plan(length):
    padded = 2 * length
    inner = LANES
    while inner * inner < 4 * padded:
        inner *= 2
    return padded, padded // inner, inner


def make_tables(length):
    padded, outer, inner = plan(length)
    ids = np.arange(inner)
    phase = 2.0 * math.pi / inner * (ids[:, None] * ids[None, :] % inner)
    cos, sin = np.cos(phase), np.sin(phase)
    forward = np.block([[cos, -sin], [sin, cos]])
    backward = np.block([[cos, sin], [-sin, cos]]) / padded * length ** (-0.5)
    turn = 2.0 * math.pi / padded * (np.arange(outer // 2 + 1)[:, None] * ids[None, :])
    turns = np.stack([np.cos(turn), np.sin(turn)])[:, :, None, :]
    turns = np.broadcast_to(turns, (2, outer // 2 + 1, SUBLANES, inner)).astype(np.float32)
    products = np.concatenate([forward, backward]).astype(np.float32)
    return products, turns


def half_fft(x):
    n = len(x)
    if n == 1:
        return [(x[0], None), (x[0], None)]
    even, odd = half_fft(x[0::2]), half_fft(x[1::2])
    bins = [None] * (n + 1)
    bins[0] = (even[0][0] + odd[0][0], None)
    bins[n] = (even[0][0] - odd[0][0], None)
    bins[n // 2] = (even[n // 2][0], -odd[n // 2][0])
    for k in range(1, n // 2):
        c, s = math.cos(math.pi * k / n), math.sin(math.pi * k / n)
        (er, ei), (orr, oi) = even[k], odd[k]
        tr = orr * c + oi * s
        ti = oi * c - orr * s
        bins[k] = (er + tr, ei + ti)
        bins[n - k] = (er - tr, ti - ei)
    return bins


def half_ifft(bins):
    n = len(bins) - 1
    if n == 1:
        return [bins[0][0] + bins[1][0]]
    even, odd = [None] * (n // 2 + 1), [None] * (n // 2 + 1)
    even[0] = (bins[0][0] + bins[n][0], None)
    odd[0] = (bins[0][0] - bins[n][0], None)
    even[n // 2] = (2.0 * bins[n // 2][0], None)
    odd[n // 2] = (-2.0 * bins[n // 2][1], None)
    for k in range(1, n // 2):
        c, s = math.cos(math.pi * k / n), math.sin(math.pi * k / n)
        (ar, ai), (br, bi) = bins[k], bins[n - k]
        even[k] = (ar + br, ai - bi)
        dr, di = ar - br, ai + bi
        odd[k] = (dr * c - di * s, dr * s + di * c)
    out = [None] * n
    out[0::2] = half_ifft(even)
    out[1::2] = half_ifft(odd)
    return out


def kernel(
    ctx,
    seqs,
    go_hbm,
    q_hbm,
    k_hbm,
    v_hbm,
    lf_hbm,
    sf_hbm,
    table_hbm,
    turn_hbm,
    gk_hbm,
    gv_hbm,
    cv_back,
    part_hbm,
    cross_in,
    gk_ref,
    gv_ref,
    go_ref,
    q_ref,
    k_ref,
    v_ref,
    lf_ref,
    sf_ref,
    table_ref,
    turn_ref,
    load_sems,
    table_split,
    taps_ref,
    d_src,
    g_src,
    sk_ref,
    gs_ref,
    d_own,
    g_own,
    gg_src,
    cv_src,
    gg_back,
    cross,
    spec_h,
    spec_d,
    spec_g,
    work,
    halo,
    send_sems,
    recv_sems,
    cross_send,
    cross_recv,
    halo_send,
    halo_recv,
    store_sems,
    keep_sems,
):
    me = lax.axis_index("ctx")
    my_seq = lax.axis_index("seq")
    chans, tok = k_ref.shape
    own = chans // ctx
    taps = sf_ref.shape[0]
    length = tok * ctx
    _, outer, inner = plan(length)
    bins = outer // 2 + 1
    chunk = work.shape[1]
    chunks = own // chunk
    per_tok = tok // inner

    def peer(off):
        return lax.rem(me + off, ctx)

    barrier = pltpu.get_barrier_semaphore()
    for off in range(1, ctx):
        pl.semaphore_signal(barrier, inc=1, device_id={"ctx": peer(off)}, device_id_type=MESH)
    for off in range(1, seqs):
        pl.semaphore_signal(
            barrier,
            inc=1,
            device_id={"seq": lax.rem(my_seq + off, seqs)},
            device_id_type=MESH,
        )
    pairs = (
        (go_hbm, go_ref),
        (q_hbm, q_ref),
        (k_hbm, k_ref),
        (sf_hbm, sf_ref),
        (v_hbm, v_ref),
        (lf_hbm, lf_ref),
        (turn_hbm, turn_ref),
        (table_hbm, table_ref),
    )
    loads = [
        pltpu.make_async_copy(src, dst, load_sems.at[i]) for i, (src, dst) in enumerate(pairs)
    ]
    for load in loads:
        load.start()
    go_load, q_load, k_load, sf_load, v_load, lf_load, turn_load, table_load = loads
    go_load.wait()
    q_load.wait()
    d_src[...] = go_ref[...] * q_ref[...]
    k_load.wait()
    halo[0] = k_ref[:, tok - LANES :].T[LANES - SUBLANES :, :]
    pl.semaphore_wait(barrier, ctx - 1 + seqs - 1)

    def halo_copy(which, off):
        return pltpu.make_async_remote_copy(
            src_ref=halo.at[2 * which],
            dst_ref=halo.at[2 * which + 1],
            send_sem=halo_send.at[which],
            recv_sem=halo_recv.at[which],
            device_id={"ctx": peer(off)},
            device_id_type=MESH,
        )

    def block(start, size):
        if isinstance(start, int):
            return pl.ds(start, size)
        return pl.ds(pl.multiple_of(start, SUBLANES), size)

    def out_copy(kind, src, dst, off, c):
        return pltpu.make_async_remote_copy(
            src_ref=src.at[block(peer(off) * own + c * chunk, chunk)],
            dst_ref=dst.at[me, pl.ds(c * chunk, chunk)],
            send_sem=send_sems.at[kind, off, c],
            recv_sem=recv_sems.at[kind, off, c],
            device_id={"ctx": peer(off)},
            device_id_type=MESH,
        )

    def back_copy(kind, src, dst, off, c):
        return pltpu.make_async_remote_copy(
            src_ref=src.at[peer(off), pl.ds(c * chunk, chunk)],
            dst_ref=dst.at[block(me * own + c * chunk, chunk)],
            send_sem=send_sems.at[kind, off, c],
            recv_sem=recv_sems.at[kind, off, c],
            device_id={"ctx": peer(off)},
            device_id_type=MESH,
        )

    def cross_copy(off, c):
        return pltpu.make_async_remote_copy(
            src_ref=cross.at[pl.ds(0, ctx), pl.ds(c * chunk, chunk)],
            dst_ref=cross_in.at[off - 1, pl.ds(0, ctx), pl.ds(c * chunk, chunk)],
            send_sem=cross_send.at[off, c],
            recv_sem=cross_recv.at[off, c],
            device_id={"seq": lax.rem(my_seq + off, seqs)},
            device_id_type=MESH,
        )

    started = []

    def start(copy):
        copy.start()
        started.append(copy)
        return copy

    key_halo = start(halo_copy(0, 1))
    d_copies = {}
    for c in range(chunks):
        for off in range(ctx - 1, 0, -1):
            d_copies[off, c] = start(out_copy(0, d_src, d_own, off, c))
    d_own[me] = d_src[block(me * own, own)]

    sf_load.wait()
    for j in range(taps):
        taps_ref[j] = jnp.broadcast_to(sf_ref[j : j + 1, :], (LANES, chans)).T

    def tap(j, rows):
        return jnp.concatenate([taps_ref[j, rows, :]] * (tok // LANES), axis=1)

    v_load.wait()
    key_halo.wait_recv()
    before = jnp.concatenate([halo[1]] * (LANES // SUBLANES), axis=0).T
    before = jnp.where(me > 0, before, 0.0)
    for z in range(ctx):
        rows = slice(z * own, (z + 1) * own)
        window = jnp.concatenate([before[rows], k_ref[rows, :]], axis=1)
        total = k_ref[rows, :] * tap(0, rows)
        for j in range(1, taps):
            total = total + pltpu.roll(window, j, 1)[:, LANES:] * tap(j, rows)
        sk_ref[rows, :] = total
        g_src[rows, :] = total * v_ref[rows, :]
    g_copies = {}
    for c in range(chunks):
        for off in range(ctx - 1, 0, -1):
            g_copies[off, c] = start(out_copy(1, g_src, g_own, off, c))
    g_own[me] = g_src[block(me * own, own)]

    def split(x):
        high = x.astype(jnp.bfloat16)
        return high, (x - high.astype(jnp.float32)).astype(jnp.bfloat16)

    def multiply(x, which):
        high, low = split(x.reshape(bins * chunk, 2 * inner))
        parts = jnp.concatenate([high, low, high], axis=1)
        y = jnp.dot(parts, table_split[which], preferred_element_type=jnp.float32)
        return y.reshape(bins, chunk, 2 * inner)

    def transform(load, c, spec):
        def rows_step(i):
            base = c * chunk + i * SUBLANES
            for lane in range(0, inner, LANES):
                x = [load(t, base, lane) for t in range(outer // 2)]
                for k, (re, im) in enumerate(half_fft(x)):
                    if k == 0:
                        re, im = re, jnp.zeros_like(re)
                    else:
                        cos = turn_ref[0, k, :, lane : lane + LANES]
                        sin = turn_ref[1, k, :, lane : lane + LANES]
                        if im is None:
                            re, im = re * cos, -re * sin
                        else:
                            re, im = re * cos + im * sin, im * cos - re * sin
                    at = block(i * SUBLANES, SUBLANES)
                    work[k, at, lane : lane + LANES] = re
                    work[k, at, inner + lane : inner + lane + LANES] = im

        for i in range(chunk // SUBLANES):
            rows_step(i)
        spec[:, c * chunk : (c + 1) * chunk, :] = multiply(work[...], 0)

    def load_from(ref):
        def load(t, base, lane):
            at = (t % per_tok) * inner + lane
            return ref[t // per_tok, block(base, SUBLANES), at : at + LANES]

        return load

    def load_filter(t, base, lane):
        at = t * inner + lane
        return lf_ref[block(base, SUBLANES), at : at + LANES]

    def product(a, b, c, conjugate):
        rows = slice(c * chunk, (c + 1) * chunk)

        ar, ai = a[:, rows, :inner], a[:, rows, inner:]
        br, bi = b[:, rows, :inner], b[:, rows, inner:]
        if conjugate:
            re, im = ar * br + ai * bi, ai * br - ar * bi
        else:
            re, im = ar * br - ai * bi, ar * bi + ai * br
        return jnp.concatenate([re, im], axis=2)

    def inverse(x, c, dst):
        work[...] = multiply(x, 1)

        def rows_step(i):
            at = block(i * SUBLANES, SUBLANES)
            for lane in range(0, inner, LANES):
                z = []
                for k in range(bins):
                    re = work[k, at, lane : lane + LANES]
                    if k == 0:
                        z.append((re, None))
                        continue
                    im = work[k, at, inner + lane : inner + lane + LANES]
                    cos = turn_ref[0, k, :, lane : lane + LANES]
                    sin = turn_ref[1, k, :, lane : lane + LANES]
                    z.append((re * cos - im * sin, re * sin + im * cos))
                for t, x in enumerate(half_ifft(z)):
                    col = (t % per_tok) * inner + lane
                    dst[t // per_tok, block(c * chunk + i * SUBLANES, SUBLANES), col : col + LANES] = x

        for i in range(chunk // SUBLANES):
            rows_step(i)

    def own_rows(c):
        return block(me * own + c * chunk, chunk)

    def chunk_rows(c):
        return pl.ds(c * chunk, chunk)

    stores = []

    def store(src, dst, sem):
        copy = pltpu.make_async_copy(src, dst, sem)
        copy.start()
        stores.append(copy)

    lf_load.wait()
    turn_load.wait()
    table_load.wait()
    for i in range(2):
        whole = table_ref[i * 2 * inner : (i + 1) * 2 * inner, :]
        high, low = split(whole)
        for part, value in enumerate((high, high, low)):
            table_split[i, part * 2 * inner : (part + 1) * 2 * inner, :] = value
    for c in range(chunks):
        transform(load_filter, c, spec_h)

    gg_copies, cv_copies, cross_copies = {}, {}, {}
    for c in range(chunks):
        for off in range(1, ctx):
            d_copies[off, c].wait_recv()
        transform(load_from(d_own), c, spec_d)
        inverse(product(spec_d, spec_h, c, True), c, gg_src)
        for off in range(ctx - 1, 0, -1):
            gg_copies[off, c] = start(back_copy(2, gg_src, gg_back, off, c))
        gg_back[own_rows(c)] = gg_src[me, chunk_rows(c)]
    for c in range(chunks):
        for off in range(1, ctx):
            g_copies[off, c].wait_recv()
        transform(load_from(g_own), c, spec_g)
        inverse(product(spec_g, spec_h, c, False), c, cv_src)
        for off in range(ctx - 1, 0, -1):
            cv_copies[off, c] = start(back_copy(3, cv_src, cv_back, off, c))
        inverse(product(spec_d, spec_g, c, True), c, cross)
        for off in range(1, seqs):
            cross_copies[off, c] = start(cross_copy(off, c))
        store(cv_src.at[me, chunk_rows(c)], cv_back.at[own_rows(c)], keep_sems.at[0, c])
        store(
            cross.at[pl.ds(0, ctx), chunk_rows(c)],
            part_hbm.at[pl.ds(0, ctx), chunk_rows(c)],
            keep_sems.at[1, c],
        )

    for copy in gg_copies.values():
        copy.wait_recv()
    grad_gated = gg_back[...]
    gs_ref[...] = grad_gated * v_ref[...]
    halo[2] = gs_ref[:, :LANES].T[:SUBLANES, :]
    head_halo = start(halo_copy(1, ctx - 1))
    gv_ref[...] = gg_back[...] * sk_ref[...]
    store(gv_ref, gv_hbm, store_sems.at[0])
    head_halo.wait_recv()
    after = jnp.concatenate([halo[3]] * (LANES // SUBLANES), axis=0).T
    after = jnp.where(me < ctx - 1, after, 0.0)
    for z in range(ctx):
        rows = slice(z * own, (z + 1) * own)
        window = jnp.concatenate([gs_ref[rows, :], after[rows]], axis=1)
        total = gs_ref[rows, :] * tap(0, rows)
        for j in range(1, taps):
            total = total + pltpu.roll(window, tok + LANES - j, 1)[:, :tok] * tap(j, rows)
        gk_ref[rows, :] = total

    store(gk_ref, gk_hbm, store_sems.at[1])

    for copy in (*cv_copies.values(), *cross_copies.values()):
        copy.wait_recv()
    for copy in stores:
        copy.wait()
    for copy in started:
        copy.wait_send()


def finish(
    gk_hbm,
    gv_hbm,
    go_hbm,
    cv_hbm,
    part_hbm,
    cross_hbm,
    gq_out,
    gk_out,
    gv_out,
    gl_out,
    gk_ref,
    gv_ref,
    go_ref,
    cv_ref,
    part_ref,
    cross_ref,
    gl_ref,
    load_sems,
    store_sems,
):
    pairs = (
        (gk_hbm, gk_ref),
        (gv_hbm, gv_ref),
        (go_hbm, go_ref),
        (cv_hbm, cv_ref),
        (part_hbm, part_ref),
        (cross_hbm, cross_ref),
    )
    loads = [
        pltpu.make_async_copy(src, dst, load_sems.at[i]) for i, (src, dst) in enumerate(pairs)
    ]
    for load in loads:
        load.start()
    stores = []

    def store(src, dst):
        copy = pltpu.make_async_copy(src, dst, store_sems.at[len(stores)])
        copy.start()
        stores.append(copy)

    loads[0].wait()
    store(gk_ref, gk_out)
    loads[1].wait()
    store(gv_ref, gv_out)
    loads[2].wait()
    loads[3].wait()
    cv_ref[...] = cv_ref[...] * go_ref[...]
    store(cv_ref, gq_out)
    loads[4].wait()
    loads[5].wait()
    ctx, _, tok = part_ref.shape
    for z in range(ctx):
        total = part_ref[z]
        for other in range(cross_ref.shape[0]):
            total = total + cross_ref[other, z]
        gl_ref[:, z * tok : (z + 1) * tok] = total
    store(gl_ref, gl_out)
    for copy in stores:
        copy.wait()


def shards(ctx, seqs, grad_out, query, keys, values, long_filter, short_filter):
    chans, tok = keys.shape[1:]
    own = chans // ctx
    length = tok * ctx
    _, outer, inner = plan(length)
    bins = outer // 2 + 1
    chunk = math.gcd(own, 16)
    chunks = own // chunk
    tables = make_tables(length)
    f32 = jnp.float32
    tokens = jax.ShapeDtypeStruct((chans, tok), f32)
    position = pltpu.VMEM((chans, tok), f32)
    channel = pltpu.VMEM((ctx, own, tok), f32)
    spectrum = pltpu.VMEM((bins, own, 2 * inner), f32)
    dma = pltpu.SemaphoreType.DMA
    operands = [x.reshape(chans, tok) for x in (grad_out, query, keys, values)]
    operands += [long_filter, short_filter.T, *(jnp.asarray(t) for t in tables)]
    hbm = pl.BlockSpec(memory_space=pltpu.HBM)
    outs = pl.pallas_call(
        functools.partial(kernel, ctx, seqs),
        out_shape=(
            tokens,
            tokens,
            tokens,
            jax.ShapeDtypeStruct((ctx, own, tok), f32),
            jax.ShapeDtypeStruct((max(seqs - 1, 1), ctx, own, tok), f32),
        ),
        in_specs=[hbm] * len(operands),
        out_specs=(hbm,) * 5,
        scratch_shapes=[
            position,
            position,
            *(pltpu.VMEM(operands[i].shape, operands[i].dtype) for i in range(len(operands))),
            dma((len(operands),)),
            pltpu.VMEM((2, 6 * inner, 2 * inner), jnp.bfloat16),
            pltpu.VMEM((short_filter.shape[1], chans, LANES), f32),
            position,
            position,
            position,
            position,
            channel,
            channel,
            channel,
            channel,
            position,
            channel,
            spectrum,
            spectrum,
            spectrum,
            pltpu.VMEM((bins, chunk, 2 * inner), f32),
            pltpu.VMEM((4, SUBLANES, chans), f32),
            dma((4, ctx, chunks)),
            dma((4, ctx, chunks)),
            dma((seqs, chunks)),
            dma((seqs, chunks)),
            dma((2,)),
            dma((2,)),
            dma((2,)),
            dma((2, chunks)),
        ],
        compiler_params=pltpu.CompilerParams(
            collective_id=0, has_side_effects=True, vmem_limit_bytes=VMEM_BYTES
        ),
    )(*operands)
    gk, gv, cv, part, cross = outs
    operands = [gk, gv, operands[0], cv, part, cross]
    result = jax.ShapeDtypeStruct((own, length), f32)
    gq, gk, gv, gl = pl.pallas_call(
        finish,
        out_shape=(tokens, tokens, tokens, result),
        in_specs=[hbm] * len(operands),
        out_specs=(hbm,) * 4,
        scratch_shapes=[
            *(pltpu.VMEM(x.shape, f32) for x in operands),
            pltpu.VMEM(result.shape, f32),
            dma((len(operands),)),
            dma((4,)),
        ],
        compiler_params=pltpu.CompilerParams(vmem_limit_bytes=VMEM_BYTES),
    )(*operands)
    return (gq[None], gk[None], gv[None], gl)


def solution(mesh):
    tokens = P("seq", "ch", "ctx")
    return jax.shard_map(
        functools.partial(shards, mesh.shape["ctx"], mesh.shape["seq"]),
        mesh=mesh,
        in_specs=(tokens, tokens, tokens, tokens, P(("ch", "ctx"), None), P("ch", None)),
        out_specs=(tokens, tokens, tokens, P(("ch", "ctx"), None)),
        check_vma=False,
    )
```

```python
import functools
import math

import jax
import jax.numpy as jnp
import numpy as np
from jax import lax
from jax.experimental import pallas as pl
from jax.experimental.pallas import tpu as pltpu
from jax.sharding import PartitionSpec as P

LANES = 128
VMEM_BYTES = 62 * 1024 * 1024
SUBLANES = 8
MESH = pl.DeviceIdType.MESH


def plan(length):
    padded = 2 * length
    inner = LANES
    while inner * inner < 4 * padded:
        inner *= 2
    return padded, padded // inner, inner


def make_tables(length):
    padded, outer, inner = plan(length)
    ids = np.arange(inner)
    phase = 2.0 * math.pi / inner * (ids[:, None] * ids[None, :] % inner)
    cos, sin = np.cos(phase), np.sin(phase)
    forward = np.block([[cos, -sin], [sin, cos]])
    backward = np.block([[cos, sin], [-sin, cos]]) / padded * length ** (-0.5)
    turn = 2.0 * math.pi / padded * (np.arange(outer // 2 + 1)[:, None] * ids[None, :])
    turns = np.stack([np.cos(turn), np.sin(turn)])[:, :, None, :]
    turns = np.broadcast_to(turns, (2, outer // 2 + 1, SUBLANES, inner)).astype(np.float32)
    products = np.concatenate([forward, backward]).astype(np.float32)
    return products, turns


def half_fft(x):
    n = len(x)
    if n == 1:
        return [(x[0], None), (x[0], None)]
    even, odd = half_fft(x[0::2]), half_fft(x[1::2])
    bins = [None] * (n + 1)
    bins[0] = (even[0][0] + odd[0][0], None)
    bins[n] = (even[0][0] - odd[0][0], None)
    bins[n // 2] = (even[n // 2][0], -odd[n // 2][0])
    for k in range(1, n // 2):
        c, s = math.cos(math.pi * k / n), math.sin(math.pi * k / n)
        (er, ei), (orr, oi) = even[k], odd[k]
        tr = orr * c + oi * s
        ti = oi * c - orr * s
        bins[k] = (er + tr, ei + ti)
        bins[n - k] = (er - tr, ti - ei)
    return bins


def half_ifft(bins):
    n = len(bins) - 1
    if n == 1:
        return [bins[0][0] + bins[1][0]]
    even, odd = [None] * (n // 2 + 1), [None] * (n // 2 + 1)
    even[0] = (bins[0][0] + bins[n][0], None)
    odd[0] = (bins[0][0] - bins[n][0], None)
    even[n // 2] = (2.0 * bins[n // 2][0], None)
    odd[n // 2] = (-2.0 * bins[n // 2][1], None)
    for k in range(1, n // 2):
        c, s = math.cos(math.pi * k / n), math.sin(math.pi * k / n)
        (ar, ai), (br, bi) = bins[k], bins[n - k]
        even[k] = (ar + br, ai - bi)
        dr, di = ar - br, ai + bi
        odd[k] = (dr * c - di * s, dr * s + di * c)
    out = [None] * n
    out[0::2] = half_ifft(even)
    out[1::2] = half_ifft(odd)
    return out


def kernel(
    ctx,
    seqs,
    go_hbm,
    q_hbm,
    k_hbm,
    v_hbm,
    lf_hbm,
    sf_hbm,
    table_hbm,
    turn_hbm,
    gk_hbm,
    gv_hbm,
    cv_back,
    part_hbm,
    cross_in,
    gk_ref,
    gv_ref,
    go_ref,
    q_ref,
    k_ref,
    v_ref,
    lf_ref,
    sf_ref,
    table_ref,
    turn_ref,
    load_sems,
    table_split,
    taps_ref,
    d_src,
    g_src,
    sk_ref,
    gs_ref,
    d_own,
    g_own,
    gg_src,
    cv_src,
    gg_back,
    cross,
    spec_h,
    spec_d,
    spec_g,
    work,
    halo,
    send_sems,
    recv_sems,
    cross_send,
    cross_recv,
    halo_send,
    halo_recv,
    store_sems,
    keep_sems,
):
    me = lax.axis_index("ctx")
    my_seq = lax.axis_index("seq")
    chans, tok = k_ref.shape
    own = chans // ctx
    taps = sf_ref.shape[0]
    length = tok * ctx
    _, outer, inner = plan(length)
    bins = outer // 2 + 1
    chunk = work.shape[1]
    chunks = own // chunk
    per_tok = tok // inner

    def peer(off):
        return lax.rem(me + off, ctx)

    barrier = pltpu.get_barrier_semaphore()
    for off in range(1, ctx):
        pl.semaphore_signal(barrier, inc=1, device_id={"ctx": peer(off)}, device_id_type=MESH)
    for off in range(1, seqs):
        pl.semaphore_signal(
            barrier,
            inc=1,
            device_id={"seq": lax.rem(my_seq + off, seqs)},
            device_id_type=MESH,
        )
    pairs = (
        (go_hbm, go_ref),
        (q_hbm, q_ref),
        (k_hbm, k_ref),
        (sf_hbm, sf_ref),
        (v_hbm, v_ref),
        (lf_hbm, lf_ref),
        (turn_hbm, turn_ref),
        (table_hbm, table_ref),
    )
    loads = [
        pltpu.make_async_copy(src, dst, load_sems.at[i]) for i, (src, dst) in enumerate(pairs)
    ]
    for load in loads:
        load.start()
    go_load, q_load, k_load, sf_load, v_load, lf_load, turn_load, table_load = loads
    go_load.wait()
    q_load.wait()
    d_src[...] = go_ref[...] * q_ref[...]
    k_load.wait()
    halo[0] = k_ref[:, tok - LANES :].T[LANES - SUBLANES :, :]
    pl.semaphore_wait(barrier, ctx - 1 + seqs - 1)

    def halo_copy(which, off):
        return pltpu.make_async_remote_copy(
            src_ref=halo.at[2 * which],
            dst_ref=halo.at[2 * which + 1],
            send_sem=halo_send.at[which],
            recv_sem=halo_recv.at[which],
            device_id={"ctx": peer(off)},
            device_id_type=MESH,
        )

    def block(start, size):
        if isinstance(start, int):
            return pl.ds(start, size)
        return pl.ds(pl.multiple_of(start, SUBLANES), size)

    def out_copy(kind, src, dst, off, c):
        return pltpu.make_async_remote_copy(
            src_ref=src.at[block(peer(off) * own + c * chunk, chunk)],
            dst_ref=dst.at[me, pl.ds(c * chunk, chunk)],
            send_sem=send_sems.at[kind, off, c],
            recv_sem=recv_sems.at[kind, off, c],
            device_id={"ctx": peer(off)},
            device_id_type=MESH,
        )

    def back_copy(kind, src, dst, off, c):
        return pltpu.make_async_remote_copy(
            src_ref=src.at[peer(off), pl.ds(c * chunk, chunk)],
            dst_ref=dst.at[block(me * own + c * chunk, chunk)],
            send_sem=send_sems.at[kind, off, c],
            recv_sem=recv_sems.at[kind, off, c],
            device_id={"ctx": peer(off)},
            device_id_type=MESH,
        )

    def cross_copy(off, c):
        return pltpu.make_async_remote_copy(
            src_ref=cross.at[pl.ds(0, ctx), pl.ds(c * chunk, chunk)],
            dst_ref=cross_in.at[off - 1, pl.ds(0, ctx), pl.ds(c * chunk, chunk)],
            send_sem=cross_send.at[off, c],
            recv_sem=cross_recv.at[off, c],
            device_id={"seq": lax.rem(my_seq + off, seqs)},
            device_id_type=MESH,
        )

    started = []

    def start(copy):
        copy.start()
        started.append(copy)
        return copy

    key_halo = start(halo_copy(0, 1))
    d_copies = {}
    for c in range(chunks):
        for off in range(ctx - 1, 0, -1):
            d_copies[off, c] = start(out_copy(0, d_src, d_own, off, c))
    d_own[me] = d_src[block(me * own, own)]

    sf_load.wait()
    for j in range(taps):
        taps_ref[j] = jnp.broadcast_to(sf_ref[j : j + 1, :], (LANES, chans)).T

    def tap(j, rows):
        return jnp.concatenate([taps_ref[j, rows, :]] * (tok // LANES), axis=1)

    v_load.wait()
    key_halo.wait_recv()
    before = jnp.concatenate([halo[1]] * (LANES // SUBLANES), axis=0).T
    before = jnp.where(me > 0, before, 0.0)
    for z in range(ctx):
        rows = slice(z * own, (z + 1) * own)
        window = jnp.concatenate([before[rows], k_ref[rows, :]], axis=1)
        total = k_ref[rows, :] * tap(0, rows)
        for j in range(1, taps):
            total = total + pltpu.roll(window, j, 1)[:, LANES:] * tap(j, rows)
        sk_ref[rows, :] = total
        g_src[rows, :] = total * v_ref[rows, :]
    g_copies = {}
    for c in range(chunks):
        for off in range(ctx - 1, 0, -1):
            g_copies[off, c] = start(out_copy(1, g_src, g_own, off, c))
    g_own[me] = g_src[block(me * own, own)]

    def split(x):
        high = x.astype(jnp.bfloat16)
        return high, (x - high.astype(jnp.float32)).astype(jnp.bfloat16)

    def multiply(x, which):
        high, low = split(x.reshape(bins * chunk, 2 * inner))
        parts = jnp.concatenate([high, low, high], axis=1)
        y = jnp.dot(parts, table_split[which], preferred_element_type=jnp.float32)
        return y.reshape(bins, chunk, 2 * inner)

    def transform(load, c, spec):
        def rows_step(i):
            base = c * chunk + i * SUBLANES
            for lane in range(0, inner, LANES):
                x = [load(t, base, lane) for t in range(outer // 2)]
                for k, (re, im) in enumerate(half_fft(x)):
                    if k == 0:
                        re, im = re, jnp.zeros_like(re)
                    else:
                        cos = turn_ref[0, k, :, lane : lane + LANES]
                        sin = turn_ref[1, k, :, lane : lane + LANES]
                        if im is None:
                            re, im = re * cos, -re * sin
                        else:
                            re, im = re * cos + im * sin, im * cos - re * sin
                    at = block(i * SUBLANES, SUBLANES)
                    work[k, at, lane : lane + LANES] = re
                    work[k, at, inner + lane : inner + lane + LANES] = im

        for i in range(chunk // SUBLANES):
            rows_step(i)
        spec[:, c * chunk : (c + 1) * chunk, :] = multiply(work[...], 0)

    def load_from(ref):
        def load(t, base, lane):
            at = (t % per_tok) * inner + lane
            return ref[t // per_tok, block(base, SUBLANES), at : at + LANES]

        return load

    def load_filter(t, base, lane):
        at = t * inner + lane
        return lf_ref[block(base, SUBLANES), at : at + LANES]

    def product(a, b, c, conjugate):
        rows = slice(c * chunk, (c + 1) * chunk)

        ar, ai = a[:, rows, :inner], a[:, rows, inner:]
        br, bi = b[:, rows, :inner], b[:, rows, inner:]
        if conjugate:
            re, im = ar * br + ai * bi, ai * br - ar * bi
        else:
            re, im = ar * br - ai * bi, ar * bi + ai * br
        return jnp.concatenate([re, im], axis=2)

    def inverse(x, c, dst):
        work[...] = multiply(x, 1)

        def rows_step(i):
            at = block(i * SUBLANES, SUBLANES)
            for lane in range(0, inner, LANES):
                z = []
                for k in range(bins):
                    re = work[k, at, lane : lane + LANES]
                    if k == 0:
                        z.append((re, None))
                        continue
                    im = work[k, at, inner + lane : inner + lane + LANES]
                    cos = turn_ref[0, k, :, lane : lane + LANES]
                    sin = turn_ref[1, k, :, lane : lane + LANES]
                    z.append((re * cos - im * sin, re * sin + im * cos))
                for t, x in enumerate(half_ifft(z)):
                    col = (t % per_tok) * inner + lane
                    dst[t // per_tok, block(c * chunk + i * SUBLANES, SUBLANES), col : col + LANES] = x

        for i in range(chunk // SUBLANES):
            rows_step(i)

    def own_rows(c):
        return block(me * own + c * chunk, chunk)

    def chunk_rows(c):
        return pl.ds(c * chunk, chunk)

    stores = []

    def store(src, dst, sem):
        copy = pltpu.make_async_copy(src, dst, sem)
        copy.start()
        stores.append(copy)

    lf_load.wait()
    turn_load.wait()
    table_load.wait()
    for i in range(2):
        whole = table_ref[i * 2 * inner : (i + 1) * 2 * inner, :]
        high, low = split(whole)
        for part, value in enumerate((high, high, low)):
            table_split[i, part * 2 * inner : (part + 1) * 2 * inner, :] = value
    for c in range(chunks):
        transform(load_filter, c, spec_h)

    gg_copies, cv_copies, cross_copies = {}, {}, {}
    for c in range(chunks):
        for off in range(1, ctx):
            d_copies[off, c].wait_recv()
        transform(load_from(d_own), c, spec_d)
        inverse(product(spec_d, spec_h, c, True), c, gg_src)
        for off in range(ctx - 1, 0, -1):
            gg_copies[off, c] = start(back_copy(2, gg_src, gg_back, off, c))
        gg_back[own_rows(c)] = gg_src[me, chunk_rows(c)]
    for c in range(chunks):
        for off in range(1, ctx):
            g_copies[off, c].wait_recv()
        transform(load_from(g_own), c, spec_g)
        inverse(product(spec_g, spec_h, c, False), c, cv_src)
        for off in range(ctx - 1, 0, -1):
            cv_copies[off, c] = start(back_copy(3, cv_src, cv_back, off, c))
        inverse(product(spec_d, spec_g, c, True), c, cross)
        for off in range(1, seqs):
            cross_copies[off, c] = start(cross_copy(off, c))
        store(cv_src.at[me, chunk_rows(c)], cv_back.at[own_rows(c)], keep_sems.at[0, c])
        store(
            cross.at[pl.ds(0, ctx), chunk_rows(c)],
            part_hbm.at[pl.ds(0, ctx), chunk_rows(c)],
            keep_sems.at[1, c],
        )

    for copy in gg_copies.values():
        copy.wait_recv()
    grad_gated = gg_back[...]
    gs_ref[...] = grad_gated * v_ref[...]
    halo[2] = gs_ref[:, :LANES].T[:SUBLANES, :]
    head_halo = start(halo_copy(1, ctx - 1))
    gv_ref[...] = gg_back[...] * sk_ref[...]
    store(gv_ref, gv_hbm, store_sems.at[0])
    head_halo.wait_recv()
    after = jnp.concatenate([halo[3]] * (LANES // SUBLANES), axis=0).T
    after = jnp.where(me < ctx - 1, after, 0.0)
    for z in range(ctx):
        rows = slice(z * own, (z + 1) * own)
        window = jnp.concatenate([gs_ref[rows, :], after[rows]], axis=1)
        total = gs_ref[rows, :] * tap(0, rows)
        for j in range(1, taps):
            total = total + pltpu.roll(window, tok + LANES - j, 1)[:, :tok] * tap(j, rows)
        gk_ref[rows, :] = total

    store(gk_ref, gk_hbm, store_sems.at[1])

    for copy in (*cv_copies.values(), *cross_copies.values()):
        copy.wait_recv()
    for copy in stores:
        copy.wait()
    for copy in started:
        copy.wait_send()


def finish(
    gk_hbm,
    gv_hbm,
    go_hbm,
    cv_hbm,
    part_hbm,
    cross_hbm,
    gq_out,
    gk_out,
    gv_out,
    gl_out,
    gk_ref,
    gv_ref,
    go_ref,
    cv_ref,
    part_ref,
    cross_ref,
    gl_ref,
    load_sems,
    store_sems,
):
    pairs = (
        (gk_hbm, gk_ref),
        (gv_hbm, gv_ref),
        (go_hbm, go_ref),
        (cv_hbm, cv_ref),
        (part_hbm, part_ref),
        (cross_hbm, cross_ref),
    )
    loads = [
        pltpu.make_async_copy(src, dst, load_sems.at[i]) for i, (src, dst) in enumerate(pairs)
    ]
    for load in loads:
        load.start()
    stores = []

    def store(src, dst):
        copy = pltpu.make_async_copy(src, dst, store_sems.at[len(stores)])
        copy.start()
        stores.append(copy)

    loads[0].wait()
    store(gk_ref, gk_out)
    loads[1].wait()
    store(gv_ref, gv_out)
    loads[2].wait()
    loads[3].wait()
    cv_ref[...] = cv_ref[...] * go_ref[...]
    store(cv_ref, gq_out)
    loads[4].wait()
    loads[5].wait()
    ctx, _, tok = part_ref.shape
    for z in range(ctx):
        total = part_ref[z]
        for other in range(cross_ref.shape[0]):
            total = total + cross_ref[other, z]
        gl_ref[:, z * tok : (z + 1) * tok] = total
    store(gl_ref, gl_out)
    for copy in stores:
        copy.wait()


def shards(ctx, seqs, grad_out, query, keys, values, long_filter, short_filter):
    chans, tok = keys.shape[1:]
    own = chans // ctx
    length = tok * ctx
    _, outer, inner = plan(length)
    bins = outer // 2 + 1
    chunk = math.gcd(own, 32)
    chunks = own // chunk
    tables = make_tables(length)
    f32 = jnp.float32
    tokens = jax.ShapeDtypeStruct((chans, tok), f32)
    position = pltpu.VMEM((chans, tok), f32)
    channel = pltpu.VMEM((ctx, own, tok), f32)
    spectrum = pltpu.VMEM((bins, own, 2 * inner), f32)
    dma = pltpu.SemaphoreType.DMA
    operands = [x.reshape(chans, tok) for x in (grad_out, query, keys, values)]
    operands += [long_filter, short_filter.T, *(jnp.asarray(t) for t in tables)]
    hbm = pl.BlockSpec(memory_space=pltpu.HBM)
    outs = pl.pallas_call(
        functools.partial(kernel, ctx, seqs),
        out_shape=(
            tokens,
            tokens,
            tokens,
            jax.ShapeDtypeStruct((ctx, own, tok), f32),
            jax.ShapeDtypeStruct((max(seqs - 1, 1), ctx, own, tok), f32),
        ),
        in_specs=[hbm] * len(operands),
        out_specs=(hbm,) * 5,
        scratch_shapes=[
            position,
            position,
            *(pltpu.VMEM(operands[i].shape, operands[i].dtype) for i in range(len(operands))),
            dma((len(operands),)),
            pltpu.VMEM((2, 6 * inner, 2 * inner), jnp.bfloat16),
            pltpu.VMEM((short_filter.shape[1], chans, LANES), f32),
            position,
            position,
            position,
            position,
            channel,
            channel,
            channel,
            channel,
            position,
            channel,
            spectrum,
            spectrum,
            spectrum,
            pltpu.VMEM((bins, chunk, 2 * inner), f32),
            pltpu.VMEM((4, SUBLANES, chans), f32),
            dma((4, ctx, chunks)),
            dma((4, ctx, chunks)),
            dma((seqs, chunks)),
            dma((seqs, chunks)),
            dma((2,)),
            dma((2,)),
            dma((2,)),
            dma((2, chunks)),
        ],
        compiler_params=pltpu.CompilerParams(
            collective_id=0, has_side_effects=True, vmem_limit_bytes=VMEM_BYTES
        ),
    )(*operands)
    gk, gv, cv, part, cross = outs
    operands = [gk, gv, operands[0], cv, part, cross]
    result = jax.ShapeDtypeStruct((own, length), f32)
    gq, gk, gv, gl = pl.pallas_call(
        finish,
        out_shape=(tokens, tokens, tokens, result),
        in_specs=[hbm] * len(operands),
        out_specs=(hbm,) * 4,
        scratch_shapes=[
            *(pltpu.VMEM(x.shape, f32) for x in operands),
            pltpu.VMEM(result.shape, f32),
            dma((len(operands),)),
            dma((4,)),
        ],
        compiler_params=pltpu.CompilerParams(vmem_limit_bytes=VMEM_BYTES),
    )(*operands)
    return (gq[None], gk[None], gv[None], gl)


def solution(mesh):
    tokens = P("seq", "ch", "ctx")
    return jax.shard_map(
        functools.partial(shards, mesh.shape["ctx"], mesh.shape["seq"]),
        mesh=mesh,
        in_specs=(tokens, tokens, tokens, tokens, P(("ch", "ctx"), None), P("ch", None)),
        out_specs=(tokens, tokens, tokens, P(("ch", "ctx"), None)),
        check_vma=False,
    )
```

```python
import functools
import math

import jax
import jax.numpy as jnp
import numpy as np
from jax import lax
from jax.experimental import pallas as pl
from jax.experimental.pallas import tpu as pltpu
from jax.sharding import PartitionSpec as P

LANES = 128
VMEM_BYTES = 62 * 1024 * 1024
SUBLANES = 8
MESH = pl.DeviceIdType.MESH


def plan(length):
    padded = 2 * length
    inner = LANES
    while inner * inner < 4 * padded:
        inner *= 2
    return padded, padded // inner, inner


def make_tables(length):
    padded, outer, inner = plan(length)
    ids = np.arange(inner)
    phase = 2.0 * math.pi / inner * (ids[:, None] * ids[None, :] % inner)
    cos, sin = np.cos(phase), np.sin(phase)
    forward = np.block([[cos, -sin], [sin, cos]])
    backward = np.block([[cos, sin], [-sin, cos]]) / padded * length ** (-0.5)
    turn = 2.0 * math.pi / padded * (np.arange(outer // 2 + 1)[:, None] * ids[None, :])
    turns = np.stack([np.cos(turn), np.sin(turn)])[:, :, None, :]
    turns = np.broadcast_to(turns, (2, outer // 2 + 1, SUBLANES, inner)).astype(np.float32)
    products = np.concatenate([forward, backward]).astype(np.float32)
    return products, turns


def half_fft(x):
    n = len(x)
    if n == 1:
        return [(x[0], None), (x[0], None)]
    even, odd = half_fft(x[0::2]), half_fft(x[1::2])
    bins = [None] * (n + 1)
    bins[0] = (even[0][0] + odd[0][0], None)
    bins[n] = (even[0][0] - odd[0][0], None)
    bins[n // 2] = (even[n // 2][0], -odd[n // 2][0])
    for k in range(1, n // 2):
        c, s = math.cos(math.pi * k / n), math.sin(math.pi * k / n)
        (er, ei), (orr, oi) = even[k], odd[k]
        tr = orr * c + oi * s
        ti = oi * c - orr * s
        bins[k] = (er + tr, ei + ti)
        bins[n - k] = (er - tr, ti - ei)
    return bins


def half_ifft(bins):
    n = len(bins) - 1
    if n == 1:
        return [bins[0][0] + bins[1][0]]
    even, odd = [None] * (n // 2 + 1), [None] * (n // 2 + 1)
    even[0] = (bins[0][0] + bins[n][0], None)
    odd[0] = (bins[0][0] - bins[n][0], None)
    even[n // 2] = (2.0 * bins[n // 2][0], None)
    odd[n // 2] = (-2.0 * bins[n // 2][1], None)
    for k in range(1, n // 2):
        c, s = math.cos(math.pi * k / n), math.sin(math.pi * k / n)
        (ar, ai), (br, bi) = bins[k], bins[n - k]
        even[k] = (ar + br, ai - bi)
        dr, di = ar - br, ai + bi
        odd[k] = (dr * c - di * s, dr * s + di * c)
    out = [None] * n
    out[0::2] = half_ifft(even)
    out[1::2] = half_ifft(odd)
    return out


def kernel(
    ctx,
    seqs,
    go_hbm,
    q_hbm,
    k_hbm,
    v_hbm,
    lf_hbm,
    sf_hbm,
    table_hbm,
    turn_hbm,
    gk_hbm,
    gv_hbm,
    cv_back,
    part_hbm,
    cross_in,
    gk_ref,
    gv_ref,
    go_ref,
    q_ref,
    k_ref,
    v_ref,
    lf_ref,
    sf_ref,
    table_ref,
    turn_ref,
    load_sems,
    table_split,
    taps_ref,
    d_src,
    g_src,
    sk_ref,
    gs_ref,
    d_own,
    g_own,
    gg_src,
    cv_src,
    gg_back,
    cross,
    spec_h,
    spec_d,
    spec_g,
    work,
    halo,
    send_sems,
    recv_sems,
    cross_send,
    cross_recv,
    halo_send,
    halo_recv,
    store_sems,
    keep_sems,
):
    me = lax.axis_index("ctx")
    my_seq = lax.axis_index("seq")
    chans, tok = k_ref.shape
    own = chans // ctx
    taps = sf_ref.shape[0]
    length = tok * ctx
    _, outer, inner = plan(length)
    bins = outer // 2 + 1
    chunk = work.shape[1]
    chunks = own // chunk
    per_tok = tok // inner

    def peer(off):
        return lax.rem(me + off, ctx)

    barrier = pltpu.get_barrier_semaphore()
    for off in range(1, ctx):
        pl.semaphore_signal(barrier, inc=1, device_id={"ctx": peer(off)}, device_id_type=MESH)
    for off in range(1, seqs):
        pl.semaphore_signal(
            barrier,
            inc=1,
            device_id={"seq": lax.rem(my_seq + off, seqs)},
            device_id_type=MESH,
        )
    pairs = (
        (go_hbm, go_ref),
        (q_hbm, q_ref),
        (k_hbm, k_ref),
        (sf_hbm, sf_ref),
        (v_hbm, v_ref),
        (lf_hbm, lf_ref),
        (turn_hbm, turn_ref),
        (table_hbm, table_ref),
    )
    loads = [
        pltpu.make_async_copy(src, dst, load_sems.at[i]) for i, (src, dst) in enumerate(pairs)
    ]
    for load in loads:
        load.start()
    go_load, q_load, k_load, sf_load, v_load, lf_load, turn_load, table_load = loads
    go_load.wait()
    q_load.wait()
    d_src[...] = go_ref[...] * q_ref[...]
    k_load.wait()
    halo[0] = k_ref[:, tok - LANES :].T[LANES - SUBLANES :, :]
    pl.semaphore_wait(barrier, ctx - 1 + seqs - 1)

    def halo_copy(which, off):
        return pltpu.make_async_remote_copy(
            src_ref=halo.at[2 * which],
            dst_ref=halo.at[2 * which + 1],
            send_sem=halo_send.at[which],
            recv_sem=halo_recv.at[which],
            device_id={"ctx": peer(off)},
            device_id_type=MESH,
        )

    def block(start, size):
        if isinstance(start, int):
            return pl.ds(start, size)
        return pl.ds(pl.multiple_of(start, SUBLANES), size)

    def out_copy(kind, src, dst, off, c):
        return pltpu.make_async_remote_copy(
            src_ref=src.at[block(peer(off) * own + c * chunk, chunk)],
            dst_ref=dst.at[me, pl.ds(c * chunk, chunk)],
            send_sem=send_sems.at[kind, off, c],
            recv_sem=recv_sems.at[kind, off, c],
            device_id={"ctx": peer(off)},
            device_id_type=MESH,
        )

    def back_copy(kind, src, dst, off, c):
        return pltpu.make_async_remote_copy(
            src_ref=src.at[peer(off), pl.ds(c * chunk, chunk)],
            dst_ref=dst.at[block(me * own + c * chunk, chunk)],
            send_sem=send_sems.at[kind, off, c],
            recv_sem=recv_sems.at[kind, off, c],
            device_id={"ctx": peer(off)},
            device_id_type=MESH,
        )

    def cross_copy(off, c):
        return pltpu.make_async_remote_copy(
            src_ref=cross.at[pl.ds(0, ctx), pl.ds(c * chunk, chunk)],
            dst_ref=cross_in.at[off - 1, pl.ds(0, ctx), pl.ds(c * chunk, chunk)],
            send_sem=cross_send.at[off, c],
            recv_sem=cross_recv.at[off, c],
            device_id={"seq": lax.rem(my_seq + off, seqs)},
            device_id_type=MESH,
        )

    started = []

    def start(copy):
        copy.start()
        started.append(copy)
        return copy

    key_halo = start(halo_copy(0, 1))
    d_copies = {}
    for c in range(chunks):
        for off in range(ctx - 1, 0, -1):
            d_copies[off, c] = start(out_copy(0, d_src, d_own, off, c))
    d_own[me] = d_src[block(me * own, own)]

    sf_load.wait()
    for j in range(taps):
        taps_ref[j] = jnp.broadcast_to(sf_ref[j : j + 1, :], (LANES, chans)).T

    def tap(j, rows):
        return jnp.concatenate([taps_ref[j, rows, :]] * (tok // LANES), axis=1)

    v_load.wait()
    key_halo.wait_recv()
    before = jnp.concatenate([halo[1]] * (LANES // SUBLANES), axis=0).T
    before = jnp.where(me > 0, before, 0.0)
    for z in range(ctx):
        rows = slice(z * own, (z + 1) * own)
        window = jnp.concatenate([before[rows], k_ref[rows, :]], axis=1)
        total = k_ref[rows, :] * tap(0, rows)
        for j in range(1, taps):
            total = total + pltpu.roll(window, j, 1)[:, LANES:] * tap(j, rows)
        sk_ref[rows, :] = total
        g_src[rows, :] = total * v_ref[rows, :]
    g_copies = {}
    for c in range(chunks):
        for off in range(ctx - 1, 0, -1):
            g_copies[off, c] = start(out_copy(1, g_src, g_own, off, c))
    g_own[me] = g_src[block(me * own, own)]

    def split(x):
        high = x.astype(jnp.bfloat16)
        return high, (x - high.astype(jnp.float32)).astype(jnp.bfloat16)

    def multiply(x, which):
        high, low = split(x.reshape(bins * chunk, 2 * inner))
        parts = jnp.concatenate([high, low, high], axis=1)
        y = jnp.dot(parts, table_split[which], preferred_element_type=jnp.float32)
        return y.reshape(bins, chunk, 2 * inner)

    def transform(load, c, spec):
        def rows_step(i):
            base = c * chunk + i * SUBLANES
            for lane in range(0, inner, LANES):
                x = [load(t, base, lane) for t in range(outer // 2)]
                for k, (re, im) in enumerate(half_fft(x)):
                    if k == 0:
                        re, im = re, jnp.zeros_like(re)
                    else:
                        cos = turn_ref[0, k, :, lane : lane + LANES]
                        sin = turn_ref[1, k, :, lane : lane + LANES]
                        if im is None:
                            re, im = re * cos, -re * sin
                        else:
                            re, im = re * cos + im * sin, im * cos - re * sin
                    at = block(i * SUBLANES, SUBLANES)
                    work[k, at, lane : lane + LANES] = re
                    work[k, at, inner + lane : inner + lane + LANES] = im

        for i in range(chunk // SUBLANES):
            rows_step(i)
        spec[:, c * chunk : (c + 1) * chunk, :] = multiply(work[...], 0)

    def load_from(ref):
        def load(t, base, lane):
            at = (t % per_tok) * inner + lane
            return ref[t // per_tok, block(base, SUBLANES), at : at + LANES]

        return load

    def load_filter(t, base, lane):
        at = t * inner + lane
        return lf_ref[block(base, SUBLANES), at : at + LANES]

    def product(a, b, c, conjugate):
        rows = slice(c * chunk, (c + 1) * chunk)

        ar, ai = a[:, rows, :inner], a[:, rows, inner:]
        br, bi = b[:, rows, :inner], b[:, rows, inner:]
        if conjugate:
            re, im = ar * br + ai * bi, ai * br - ar * bi
        else:
            re, im = ar * br - ai * bi, ar * bi + ai * br
        return jnp.concatenate([re, im], axis=2)

    def inverse(x, c, dst):
        work[...] = multiply(x, 1)

        def rows_step(i):
            at = block(i * SUBLANES, SUBLANES)
            for lane in range(0, inner, LANES):
                z = []
                for k in range(bins):
                    re = work[k, at, lane : lane + LANES]
                    if k == 0:
                        z.append((re, None))
                        continue
                    im = work[k, at, inner + lane : inner + lane + LANES]
                    cos = turn_ref[0, k, :, lane : lane + LANES]
                    sin = turn_ref[1, k, :, lane : lane + LANES]
                    z.append((re * cos - im * sin, re * sin + im * cos))
                for t, x in enumerate(half_ifft(z)):
                    col = (t % per_tok) * inner + lane
                    dst[t // per_tok, block(c * chunk + i * SUBLANES, SUBLANES), col : col + LANES] = x

        for i in range(chunk // SUBLANES):
            rows_step(i)

    def own_rows(c):
        return block(me * own + c * chunk, chunk)

    def chunk_rows(c):
        return pl.ds(c * chunk, chunk)

    stores = []

    def store(src, dst, sem):
        copy = pltpu.make_async_copy(src, dst, sem)
        copy.start()
        stores.append(copy)

    lf_load.wait()
    turn_load.wait()
    table_load.wait()
    for i in range(2):
        whole = table_ref[i * 2 * inner : (i + 1) * 2 * inner, :]
        high, low = split(whole)
        for part, value in enumerate((high, high, low)):
            table_split[i, part * 2 * inner : (part + 1) * 2 * inner, :] = value
    for c in range(chunks):
        transform(load_filter, c, spec_h)

    gg_copies, cv_copies, cross_copies = {}, {}, {}
    for c in range(chunks):
        for off in range(1, ctx):
            d_copies[off, c].wait_recv()
        transform(load_from(d_own), c, spec_d)
        inverse(product(spec_d, spec_h, c, True), c, gg_src)
        gg_back[own_rows(c)] = gg_src[me, chunk_rows(c)]
    for c in range(chunks):
        for off in range(1, ctx):
            if off == ctx - 1:
                for back in range(ctx - 1, 0, -1):
                    gg_copies[back, c] = start(back_copy(2, gg_src, gg_back, back, c))
            g_copies[off, c].wait_recv()
        transform(load_from(g_own), c, spec_g)
        inverse(product(spec_g, spec_h, c, False), c, cv_src)
        for off in range(ctx - 1, 0, -1):
            cv_copies[off, c] = start(back_copy(3, cv_src, cv_back, off, c))
        inverse(product(spec_d, spec_g, c, True), c, cross)
        for off in range(1, seqs):
            cross_copies[off, c] = start(cross_copy(off, c))
        store(cv_src.at[me, chunk_rows(c)], cv_back.at[own_rows(c)], keep_sems.at[0, c])
        store(
            cross.at[pl.ds(0, ctx), chunk_rows(c)],
            part_hbm.at[pl.ds(0, ctx), chunk_rows(c)],
            keep_sems.at[1, c],
        )

    for copy in gg_copies.values():
        copy.wait_recv()
    grad_gated = gg_back[...]
    gs_ref[...] = grad_gated * v_ref[...]
    halo[2] = gs_ref[:, :LANES].T[:SUBLANES, :]
    head_halo = start(halo_copy(1, ctx - 1))
    gv_ref[...] = gg_back[...] * sk_ref[...]
    store(gv_ref, gv_hbm, store_sems.at[0])
    head_halo.wait_recv()
    after = jnp.concatenate([halo[3]] * (LANES // SUBLANES), axis=0).T
    after = jnp.where(me < ctx - 1, after, 0.0)
    for z in range(ctx):
        rows = slice(z * own, (z + 1) * own)
        window = jnp.concatenate([gs_ref[rows, :], after[rows]], axis=1)
        total = gs_ref[rows, :] * tap(0, rows)
        for j in range(1, taps):
            total = total + pltpu.roll(window, tok + LANES - j, 1)[:, :tok] * tap(j, rows)
        gk_ref[rows, :] = total

    store(gk_ref, gk_hbm, store_sems.at[1])

    for copy in (*cv_copies.values(), *cross_copies.values()):
        copy.wait_recv()
    for copy in stores:
        copy.wait()
    for copy in started:
        copy.wait_send()


def finish(
    gk_hbm,
    gv_hbm,
    go_hbm,
    cv_hbm,
    part_hbm,
    cross_hbm,
    gq_out,
    gk_out,
    gv_out,
    gl_out,
    gk_ref,
    gv_ref,
    go_ref,
    cv_ref,
    part_ref,
    cross_ref,
    gl_ref,
    load_sems,
    store_sems,
):
    pairs = (
        (gk_hbm, gk_ref),
        (gv_hbm, gv_ref),
        (go_hbm, go_ref),
        (cv_hbm, cv_ref),
        (part_hbm, part_ref),
        (cross_hbm, cross_ref),
    )
    loads = [
        pltpu.make_async_copy(src, dst, load_sems.at[i]) for i, (src, dst) in enumerate(pairs)
    ]
    for load in loads:
        load.start()
    stores = []

    def store(src, dst):
        copy = pltpu.make_async_copy(src, dst, store_sems.at[len(stores)])
        copy.start()
        stores.append(copy)

    loads[0].wait()
    store(gk_ref, gk_out)
    loads[1].wait()
    store(gv_ref, gv_out)
    loads[2].wait()
    loads[3].wait()
    cv_ref[...] = cv_ref[...] * go_ref[...]
    store(cv_ref, gq_out)
    loads[4].wait()
    loads[5].wait()
    ctx, _, tok = part_ref.shape
    for z in range(ctx):
        total = part_ref[z]
        for other in range(cross_ref.shape[0]):
            total = total + cross_ref[other, z]
        gl_ref[:, z * tok : (z + 1) * tok] = total
    store(gl_ref, gl_out)
    for copy in stores:
        copy.wait()


def shards(ctx, seqs, grad_out, query, keys, values, long_filter, short_filter):
    chans, tok = keys.shape[1:]
    own = chans // ctx
    length = tok * ctx
    _, outer, inner = plan(length)
    bins = outer // 2 + 1
    chunk = math.gcd(own, 32)
    chunks = own // chunk
    tables = make_tables(length)
    f32 = jnp.float32
    tokens = jax.ShapeDtypeStruct((chans, tok), f32)
    position = pltpu.VMEM((chans, tok), f32)
    channel = pltpu.VMEM((ctx, own, tok), f32)
    spectrum = pltpu.VMEM((bins, own, 2 * inner), f32)
    dma = pltpu.SemaphoreType.DMA
    operands = [x.reshape(chans, tok) for x in (grad_out, query, keys, values)]
    operands += [long_filter, short_filter.T, *(jnp.asarray(t) for t in tables)]
    hbm = pl.BlockSpec(memory_space=pltpu.HBM)
    outs = pl.pallas_call(
        functools.partial(kernel, ctx, seqs),
        out_shape=(
            tokens,
            tokens,
            tokens,
            jax.ShapeDtypeStruct((ctx, own, tok), f32),
            jax.ShapeDtypeStruct((max(seqs - 1, 1), ctx, own, tok), f32),
        ),
        in_specs=[hbm] * len(operands),
        out_specs=(hbm,) * 5,
        scratch_shapes=[
            position,
            position,
            *(pltpu.VMEM(operands[i].shape, operands[i].dtype) for i in range(len(operands))),
            dma((len(operands),)),
            pltpu.VMEM((2, 6 * inner, 2 * inner), jnp.bfloat16),
            pltpu.VMEM((short_filter.shape[1], chans, LANES), f32),
            position,
            position,
            position,
            position,
            channel,
            channel,
            channel,
            channel,
            position,
            channel,
            spectrum,
            spectrum,
            spectrum,
            pltpu.VMEM((bins, chunk, 2 * inner), f32),
            pltpu.VMEM((4, SUBLANES, chans), f32),
            dma((4, ctx, chunks)),
            dma((4, ctx, chunks)),
            dma((seqs, chunks)),
            dma((seqs, chunks)),
            dma((2,)),
            dma((2,)),
            dma((2,)),
            dma((2, chunks)),
        ],
        compiler_params=pltpu.CompilerParams(
            collective_id=0, has_side_effects=True, vmem_limit_bytes=VMEM_BYTES
        ),
    )(*operands)
    gk, gv, cv, part, cross = outs
    operands = [gk, gv, operands[0], cv, part, cross]
    result = jax.ShapeDtypeStruct((own, length), f32)
    gq, gk, gv, gl = pl.pallas_call(
        finish,
        out_shape=(tokens, tokens, tokens, result),
        in_specs=[hbm] * len(operands),
        out_specs=(hbm,) * 4,
        scratch_shapes=[
            *(pltpu.VMEM(x.shape, f32) for x in operands),
            pltpu.VMEM(result.shape, f32),
            dma((len(operands),)),
            dma((4,)),
        ],
        compiler_params=pltpu.CompilerParams(vmem_limit_bytes=VMEM_BYTES),
    )(*operands)
    return (gq[None], gk[None], gv[None], gl)


def solution(mesh):
    tokens = P("seq", "ch", "ctx")
    return jax.shard_map(
        functools.partial(shards, mesh.shape["ctx"], mesh.shape["seq"]),
        mesh=mesh,
        in_specs=(tokens, tokens, tokens, tokens, P(("ch", "ctx"), None), P("ch", None)),
        out_specs=(tokens, tokens, tokens, P(("ch", "ctx"), None)),
        check_vma=False,
    )
```
